128 devices in a mesh: group: 8 (over y_hi, x), replica: 16 (over y_lo, z, core).
Axes of the slice: x: 4, y: 4 (y_hi: 2, y_lo: 2; y = y_hi * 2 + y_lo), z: 4, core: 2. Of those that a mesh axis runs over, the one named last changes fastest.
Arguments:
- hidden_in: bfloat16 [16, 1024, 1536], P('replica', 'group'), may hold values from -6 to 6
- norm_attn: bfloat16 [1536], P('group'), may hold values from 0.099609375 to 1.8984375
- w_qkv: bfloat16 [1536, 2048], P('group'), may hold values from -0.15625 to 0.15625
- b_qkv: bfloat16 [2048], P('group'), may hold values from -3 to 3
- w_out: bfloat16 [1536, 1536], P('group'), may hold values from -0.625 to 0.625
- norm_mlp: bfloat16 [1536], P('group'), may hold values from 0.099609375 to 1.8984375
- w_gate_up: bfloat16 [1536, 17920], P('group'), may hold values from -0.15625 to 0.15625
- w_down: bfloat16 [8960, 1536], P('group'), may hold values from -0.09375 to 0.09375
- cotangent: bfloat16 [16, 1024, 1536], P('replica', 'group'), may hold values from -6 to 6
Outputs:
- hidden_out: bfloat16 [16, 1024, 1536], P('replica', 'group')
- grad_in: float32 [16, 1024, 1536], P('replica', 'group')
- grad_norm_attn: float32 [1536], P('group')
- grad_w_qkv: float32 [1536, 2048], P('group')
- grad_b_qkv: float32 [2048], P('group')
- grad_w_out: float32 [1536, 1536], P('group')
- grad_norm_mlp: float32 [1536], P('group')
- grad_w_gate_up: float32 [1536, 17920], P('group')
- grad_w_down: float32 [8960, 1536], P('group')
The draws below stay inside these ranges and needn't reach their ends.
All inputs are finite; a program needn't handle non-finite values.
Results may differ from the reference program's by a relative error of at most 0.025.
Values may be sent and summed in bfloat16 or wider, within the bound.
No kernel may reach another device: no remote copies, remote signals or barrier semaphores. Data moves between devices by JAX's collectives and lax.ppermute only.
A program may use at most 320 MiB of HBM per device.

```python
import jax
import jax.numpy as jnp
from jax import lax

D = 1536
HEADS = 12
KV_HEADS = 2
HEAD = 128
FF = 8960
LEN = 1024
SEQS = 16
QKV = 2048


def steps_of(key, extent, pieces, low, largest):
    factor_of = 1.0
    for axis_at, parts in pieces:
        draws = jax.random.uniform(jax.random.fold_in(jax.random.fold_in(key, 6), axis_at), (parts,), jnp.float32, low / len(pieces), largest / len(pieces))
        factor_of = factor_of * jnp.repeat(jnp.exp(draws), extent[axis_at] // parts).reshape((-1,) + (1,) * (len(extent) - 1 - axis_at))
    return factor_of


def normal_values(rng, dims, spread, limit, cuts=(), kind=jnp.bfloat16):
    array = spread * jax.random.normal(rng, dims, jnp.float32)
    if cuts:
        array = array * steps_of(rng, dims, cuts, -0.22, 0.18)
    return jnp.clip(array, -limit, limit).astype(kind)


def setup_inputs(seed: int = 0) -> dict:
    splits = jax.random.split(jax.random.key(seed), 10)
    hidden_in = normal_values(splits[0], (SEQS, LEN, D), 1.0, 6.0, ((0, 16), (1, 8)))
    norm_attn = jnp.clip(1.0 + 0.18 * jax.random.normal(splits[1], (D,), jnp.float32), 0.099609375, 1.8984375).astype(jnp.bfloat16)
    w_qkv = normal_values(splits[2], (D, QKV), D ** -0.5, 0.15625, ((0, 8),))
    b_qkv = normal_values(splits[3], (QKV,), 0.5, 3.0, ((0, 8),))
    w_out = normal_values(splits[4], (HEADS * HEAD, D), (HEADS * HEAD // 16) ** -0.5, 0.625, ((0, 8),))
    norm_mlp = jnp.clip(1.0 + 0.18 * jax.random.normal(splits[5], (D,), jnp.float32), 0.099609375, 1.8984375).astype(jnp.bfloat16)
    w_gate_up = normal_values(splits[6], (D, 2 * FF), D ** -0.5, 0.15625, ((0, 8),))
    w_down = normal_values(splits[7], (FF, D), (FF // 2) ** -0.5, 0.09375, ((0, 8),))
    cotangent = normal_values(splits[8], (SEQS, LEN, D), 1.0, 6.0, ((0, 16), (1, 8)))
    return dict(hidden_in=hidden_in, norm_attn=norm_attn, w_qkv=w_qkv, b_qkv=b_qkv, w_out=w_out, norm_mlp=norm_mlp, w_gate_up=w_gate_up, w_down=w_down, cotangent=cotangent)


@jax.custom_vjp
def low(v):
    return lax.optimization_barrier(v.astype(jnp.bfloat16)).astype(jnp.float32)

@jax.custom_vjp
def low_back(v):
    return v

def low_keep(v):
    return (low(v), None)

def low_pass(kept, grad):
    return (grad,)

def back_keep(v):
    return (v, None)

def back_low(kept, grad):
    return (low(grad),)
low.defvjp(low_keep, low_pass)
low_back.defvjp(back_keep, back_low)
NORM_EPSILON = 1e-06
ROPE_BASE = 1000000.0

def rope_tables(first_row, row_count, head_size):
    half_width = head_size // 2
    position = (first_row + jnp.arange(row_count)).astype(jnp.float32)
    frequency = jnp.power(ROPE_BASE, -(jnp.arange(half_width).astype(jnp.float32) * 2.0) / head_size)
    angles = position[:, None] * frequency[None, :]
    cosine = jnp.concatenate([jnp.cos(angles), jnp.cos(angles)], axis=-1)
    sine_part = jnp.concatenate([jnp.sin(angles), jnp.sin(angles)], axis=-1)
    return (cosine[:, None, :], sine_part[:, None, :])

def turn(vectors, cosine, sine_part):
    half_width = vectors.shape[-1] // 2
    swapped = jnp.concatenate([-vectors[..., half_width:], vectors[..., :half_width]], axis=-1)
    return vectors * cosine + swapped * sine_part

def forward(rows_in, gain_one, w_qkv, b_qkv, w_out, gain_two, w_gate_up, w_down):
    highest = lax.Precision.HIGHEST
    length = rows_in.shape[0]
    width_q = HEADS * HEAD
    width_k = KV_HEADS * HEAD
    groups = HEADS // KV_HEADS
    scale_one = lax.rsqrt(lax.optimization_barrier(jnp.mean(rows_in * rows_in, axis=-1, keepdims=True)) + NORM_EPSILON)
    normed_one = low(rows_in * scale_one * gain_one)
    projected = low_back(jnp.dot(normed_one, w_qkv, precision=highest) + b_qkv)
    cosine, sine_part = rope_tables(0, length, HEAD)
    queries = low(turn(projected[:, :width_q].reshape(length, HEADS, HEAD), cosine, sine_part))
    keys_all = low(turn(projected[:, width_q:width_q + width_k].reshape(length, KV_HEADS, HEAD), cosine, sine_part))
    values = low(projected[:, width_q + width_k:].reshape(length, KV_HEADS, HEAD))
    grouped = queries.reshape(length, KV_HEADS, groups, HEAD)
    raw_scores = jnp.einsum('qkgd,skd->kgqs', grouped, keys_all, precision=highest)
    scores = low_back(raw_scores * HEAD ** (-0.5))
    allowed = jnp.arange(length)[:, None] >= jnp.arange(length)[None, :]
    scores = jnp.where(allowed, scores, -1e+30)
    attn_probs = jax.nn.softmax(scores, axis=-1)
    mixed = jnp.einsum('kgqs,skd->qkgd', low(attn_probs), values, precision=highest).reshape(length, width_q)
    attended = low(low_back(mixed))
    middle = rows_in + low_back(jnp.dot(attended, w_out, precision=highest))
    scale_two = lax.rsqrt(lax.optimization_barrier(jnp.mean(middle * middle, axis=-1, keepdims=True)) + NORM_EPSILON)
    normed_two = low(middle * scale_two * gain_two)
    gate_up = low_back(jnp.dot(normed_two, w_gate_up, precision=highest))
    activated = low(jax.nn.silu(gate_up[:, :FF]) * gate_up[:, FF:])
    return middle + low_back(jnp.dot(activated, w_down, precision=highest))

def reference(hidden_in, norm_attn, w_qkv, b_qkv, w_out, norm_mlp, w_gate_up, w_down, cotangent):
    params = (norm_attn.astype(jnp.float32), w_qkv.astype(jnp.float32), b_qkv.astype(jnp.float32), w_out.astype(jnp.float32), norm_mlp.astype(jnp.float32), w_gate_up.astype(jnp.float32), w_down.astype(jnp.float32))

    def one_sequence(totals, seq_pair):
        rows_in, grad_rows = seq_pair
        seq_out, pullback = jax.vjp(forward, rows_in, *params)
        seq_grads = pullback(grad_rows)
        totals = tuple((left_sum + right_sum for left_sum, right_sum in zip(totals, seq_grads[1:])))
        return (totals, (seq_out.astype(jnp.bfloat16), seq_grads[0]))
    zero_sums = tuple((jnp.zeros(param.shape, jnp.float32) for param in params))
    totals, (outputs, grad_in) = lax.scan(one_sequence, zero_sums, (hidden_in.astype(jnp.float32), cotangent.astype(jnp.float32)))
    return (outputs, grad_in, totals[0], totals[1], totals[2], totals[3], totals[4], totals[5], totals[6])
```

```python
import functools

import jax
import jax.numpy as jnp
from jax import lax
from jax.experimental import pallas as pl
from jax.experimental.pallas import tpu as pltpu
from jax.sharding import Mesh, PartitionSpec as P

D = 1536
HEADS = 12
KV_HEADS = 2
HEAD = 128
FF = 8960
QKV = 2048
ROWS = 128
GROUPS = HEADS // KV_HEADS
WIDTH_Q = HEADS * HEAD
WIDTH_K = KV_HEADS * HEAD
ROLES = 14
COLS = FF // ROLES
SHARD = D // 8
PIECE = COLS // 8
PIECES = FF // 8 // PIECE

NORM_EPSILON = 1e-06
ROPE_BASE = 1000000.0
BF = jnp.bfloat16


def cost(micros):
    return pl.CostEstimate(flops=int(micros * SCALE), bytes_accessed=1000, transcendentals=0)


SCALE = 0.58e9
F32 = jnp.float32

GROUP = ("yh", "x")
PLANE = ("yl", "z")
REPLICA = ("yl", "z", "c")
GROUP_CORE = ("yh", "x", "c")
EVERY = ("yh", "x", "yl", "z", "c")

ALL_OFFSETS = ((0, 0), (0, 1), (0, 3), (1, 0), (0, 2), (1, 1), (1, 3), (1, 2))


def shift_pairs(offset):
    dy, dx = offset
    return [
        (y * 4 + x, ((y + dy) % 2) * 4 + (x + dx) % 4) for y in range(2) for x in range(4)
    ]


def back(offset):
    return (offset[0], (4 - offset[1]) % 4)


def send(block, axes, offset):
    return lax.ppermute(block, axes, shift_pairs(offset))


def send_out(block, axes):
    one, three = send(block, axes, (0, 1)), send(block, axes, (0, 3))
    across, two = send(block, axes, (1, 0)), send(block, axes, (0, 2))
    return [
        block,
        one,
        three,
        across,
        two,
        send(across, axes, (0, 1)),
        send(across, axes, (0, 3)),
        send(two, axes, (1, 0)),
    ]


def send_parts(blocks, axes, hold=()):
    first = (
        send(blocks[1, 1], axes, (0, 1)),
        send(blocks[1, 3], axes, (0, 3)),
        send(blocks[1, 2], axes, (1, 0)),
    )
    from_one, from_three, from_across = after(first, *hold)
    two = (blocks[0, 2].astype(F32) + from_across.astype(F32)).astype(BF)
    across = total([blocks[1, 0], from_one, from_three]).astype(BF)
    parts = [
        blocks[0, 0],
        send(blocks[0, 1], axes, (0, 1)),
        send(blocks[0, 3], axes, (0, 3)),
        send(two, axes, (0, 2)),
        send(across, axes, (1, 0)),
    ]
    return parts, first, (two, across)


def after(value, *done):
    return lax.optimization_barrier((value,) + done)[0] if done else value


def total(blocks):
    out = blocks[0].astype(F32)
    for b in blocks[1:]:
        out = out + b.astype(F32)
    return out


def down_pairs():
    pairs = []
    for r in range(ROLES):
        for g in range(8):
            piece = 8 * r + g
            pairs.append(((piece // PIECES) * 16 + piece % PIECES, g * 16 + r))
    return pairs


def rope_tables(first_row, row_count, head_size):
    half_width = head_size // 2
    position = (first_row + jnp.arange(row_count, dtype=jnp.int32)).astype(F32)
    frequency = jnp.power(
        ROPE_BASE, -(jnp.arange(half_width, dtype=jnp.int32).astype(F32) * 2.0) / head_size
    )
    angles = position[:, None] * frequency[None, :]
    cosine = jnp.concatenate([jnp.cos(angles), jnp.cos(angles)], axis=-1)
    signed = jnp.concatenate([-jnp.sin(angles), jnp.sin(angles)], axis=-1)
    return (cosine, signed)


def contract_rows(left_side, right_side):
    return lax.dot_general(
        left_side, right_side, (((0,), (0,)), ((), ())), preferred_element_type=F32
    )


def contract_cols(left_side, right_side):
    return lax.dot_general(
        left_side, right_side, (((1,), (1,)), ((), ())), preferred_element_type=F32
    )


def swap(block):
    return lax.ppermute(block, "c", [(0, 1), (1, 0)])


def gather_direct(block, axes):
    return lax.all_to_all(jnp.broadcast_to(block[None], (8,) + block.shape), axes, 0, 0, tiled=True)


def place(y, x, offset, sign=1):
    return ((y + sign * offset[0]) % 2) * 4 + (x + sign * offset[1]) % 4


def pick(blocks, index):
    return lax.dynamic_index_in_dim(blocks, index, 0, keepdims=False)


def piece_parts():
    for i in range(5):
        for j in range(6):
            low, high = max(96 * i, 80 * j), min(96 * (i + 1), 80 * (j + 1))
            if low < high:
                yield (
                    (slice(low - 96 * i, high - 96 * i), slice(256 * i, 256 * (i + 1))),
                    (slice(low - 80 * j, high - 80 * j), slice(256 * j, 256 * (j + 1))),
                )


def call(kernel, micros, out_shape, in_specs, *args, vmem=48, **more):
    return pl.pallas_call(
        kernel,
        in_specs=in_specs,
        out_specs=[pl.BlockSpec(memory_space=pltpu.VMEM)] * len(out_shape),
        out_shape=[jax.ShapeDtypeStruct(shape, kind) for shape, kind in out_shape],
        compiler_params=pltpu.CompilerParams(vmem_limit_bytes=vmem << 20),
        cost_estimate=cost(micros),
        **more,
    )(*args)


def pack_kernel(works_ref, gate_ref, up_ref, piece_ref, out_ref):
    works = works_ref[0] > 0
    gate, up = gate_ref[...], up_ref[...]
    out_ref[:SHARD, :COLS] = jnp.where(works, gate, jnp.zeros_like(gate))
    out_ref[:SHARD, COLS:] = jnp.where(works, up, jnp.zeros_like(up))
    for (r, c), (rows, cols) in piece_parts():
        out_ref[SHARD + r.start : SHARD + r.stop, c] = piece_ref[rows, cols]


def arrange_kernel(order_ref, *refs):
    for k in range(8):
        refs[8][order_ref[k]] = refs[k][...]


def arrange(order, blocks):
    return call(
        arrange_kernel,
        2,
        [((8,) + blocks[0].shape, BF)],
        [pl.BlockSpec(memory_space=pltpu.SMEM)] + whole(8),
        order,
        *blocks,
    )[0]


def packed_grads(order_ref, refs, up_sum, down_sum, scratch):
    h_all, c_all, grad, act, sems = scratch
    c_ref, grad_ref, act_ref = refs[8:11]
    copies = fetch(
        [(grad_ref, grad)]
        + [(refs[k], rows_of(h_all, k)) for k in range(8)]
        + [(act_ref, act)]
        + [(c_ref.at[order_ref[k]], rows_of(c_all, k)) for k in range(8)],
        sems,
    )
    for copy in copies[:9]:
        copy.wait()
    up_sum[...] = contract_rows(h_all[...], grad[...]).reshape(8, SHARD, 2 * COLS).astype(BF)
    for copy in copies[9:]:
        copy.wait()
    down_sum[...] = contract_rows(act[...], c_all[...]).astype(BF)


GRAD_SCRATCH = [
    pltpu.VMEM((8 * ROWS, D), BF),
    pltpu.VMEM((8 * ROWS, D), BF),
    pltpu.VMEM((8 * ROWS, 2 * COLS), BF),
    pltpu.VMEM((8 * ROWS, COLS), BF),
    pltpu.SemaphoreType.DMA((18,)),
]


def weight_kernel(order_ref, *refs):
    out_ref, down_sum = refs[11:13]
    packed_grads(order_ref, refs, out_ref.at[:, :SHARD], down_sum, refs[13:])
    for g in range(8):
        for (r, c), (rows, cols) in piece_parts():
            out_ref[g, SHARD + r.start : SHARD + r.stop, c] = down_sum[
                PIECE * g + rows.start : PIECE * g + rows.stop, cols
            ]


def weight_grads(order, h_blocks, cot_all, grads, acts):
    return call(
        weight_kernel,
        10.7,
        [((8, SHARD + 96, 2 * COLS), BF)],
        scalars(1) + anywhere(11),
        order,
        *h_blocks,
        cot_all,
        grads,
        acts,
        scratch_shapes=[pltpu.VMEM((COLS, D), BF)] + GRAD_SCRATCH,
    )[0]


def merge_kernel(token_order_ref, order_ref, *refs):
    given_ref, outs, (up_sum, down_sum, given, sem) = refs[11], refs[12:20], refs[20:24]
    copy = fetch([(given_ref, given)], sem)[0]
    packed_grads(token_order_ref, refs, up_sum, down_sum, refs[24:])
    copy.wait()
    for k in range(8):
        g = order_ref[k]
        outs[k][:SHARD] = (up_sum[g].astype(F32) + given[g, :SHARD].astype(F32)).astype(BF)
        first = pl.multiple_of(g * PIECE, PIECE)
        for (r, c), (rows, cols) in piece_parts():
            to = slice(SHARD + r.start, SHARD + r.stop)
            own = down_sum[pl.ds(first + rows.start, rows.stop - rows.start), cols]
            outs[k][to, c] = (own.astype(F32) + given[g, to, c].astype(F32)).astype(BF)


def merged_grads(token_order, order, h_blocks, cot_all, grads, acts, given):
    return call(
        merge_kernel,
        15,
        [((SHARD + 96, 2 * COLS), BF)] * 8,
        scalars(2) + anywhere(12),
        token_order,
        order,
        *h_blocks,
        cot_all,
        grads,
        acts,
        given,
        vmem=56,
        scratch_shapes=[
            pltpu.VMEM((8, SHARD, 2 * COLS), BF),
            pltpu.VMEM((COLS, D), BF),
            pltpu.VMEM((8, SHARD + 96, 2 * COLS), BF),
            pltpu.SemaphoreType.DMA((1,)),
        ]
        + GRAD_SCRATCH,
    )


def finish_kernel(
    core_ref, grad_ref, mine_ref, other_ref, x_ref, gain_ref, mid_ref, out_ref, gain_grad_ref
):
    half = QKV // 2
    grad = grad_ref[...]
    mine, other = halves(core_ref, grad[:, :half], grad[:, half:])
    normed = contract_cols(mine, mine_ref[...]) + contract_cols(other, other_ref[...])
    x = x_ref[...].astype(F32)
    scale = lax.rsqrt(jnp.mean(x * x, axis=-1, keepdims=True) + NORM_EPSILON)
    gain_grad_ref[...] = jnp.sum(normed * x * scale, axis=0, keepdims=True)
    weighted = normed * gain_ref[...]
    mean = jnp.mean(weighted * x, axis=-1, keepdims=True)
    out_ref[...] = mid_ref[...] + scale * (weighted - x * (scale * scale * mean))


def finish(core, grad_projected, mine, other, rows, gain, grad_middle):
    return call(
        finish_kernel, 5,
        [((ROWS, D), F32), ((1, D), F32)],
        [pl.BlockSpec(memory_space=pltpu.SMEM)] + whole(6),
        core,
        grad_projected,
        mine,
        other,
        rows,
        gain,
        grad_middle,
    )


def attention_grads_kernel(core_ref, normed_ref, att_ref, both_ref, keep_ref, give_ref, bias_ref):
    both = both_ref[...].reshape(8 * ROWS, 512)
    role = both[:, :256]
    bias_ref[...] = jnp.sum(role.astype(F32), axis=0, keepdims=True)
    qkv = contract_rows(normed_ref[...].reshape(8 * ROWS, D), role)
    out = contract_rows(att_ref[...].reshape(8 * ROWS, D), both[:, 256:])
    keep, give = halves(core_ref, qkv, out)
    keep_ref[...] = keep
    give_ref[...] = give.astype(BF)


def attention_grads(core, normed, attended, both):
    return call(
        attention_grads_kernel,
        5,
        [((D, 256), F32), ((D, 256), BF), ((1, 256), F32)],
        [pl.BlockSpec(memory_space=pltpu.SMEM)] + whole(3),
        core,
        normed,
        attended,
        both,
    )


def last_kernel(core_ref, group_ref, mine_ref, other_ref, qkv_ref, out_ref, gain_ref, bias_ref):
    gains = jnp.zeros((16, 256), F32)
    for q in range(8):
        mine, other = mine_ref[q].astype(F32), other_ref[q].astype(F32)
        qkv, out = halves(core_ref, mine[:SHARD], other[:SHARD])
        qkv_ref[:, 256 * q : 256 * (q + 1)] = qkv
        if q < 6:
            out_ref[:, 256 * q : 256 * (q + 1)] = out
        gains = gains + mine[SHARD:] + other[SHARD:]
    gain_ref[...] = gains
    g = group_ref[0]
    bias_ref[...] = mine_ref[g, SHARD:].astype(F32) + other_ref[g, SHARD:].astype(F32)


def payload_kernel(keep_ref, other_ref, extra_ref, bias_ref, out_ref):
    row = lax.broadcasted_iota(jnp.int32, (16, 256), 0)
    bias = bias_ref[...].astype(BF).astype(F32)
    for g in range(8):
        rows = slice(SHARD * g, SHARD * (g + 1))
        out_ref[g, :SHARD] = (keep_ref[rows] + other_ref[rows].astype(F32)).astype(BF)
        extra = extra_ref[g].astype(F32)
        out_ref[g, SHARD:] = jnp.where(row == 2, bias, extra).astype(BF)


def sum_kernel(in_ref, out_ref):
    rows = in_ref[0].astype(F32)
    for g in range(1, 8):
        rows = rows + in_ref[g].astype(F32)
    rows = rows.astype(BF)
    for g in range(8):
        out_ref[g] = rows


def write_kernel(low, count, held, core_ref, order_ref, *refs):
    blocks = refs[: 2 * count]
    wide_out, down_out, narrow, wide, down, in_sems, sems = refs[2 * count + held :]
    arrivals = fetch([(blocks[n], narrow.at[n]) for n in range(2 * count)], in_sems)
    for start in (True, False):
        for n in range(2 * count):
            chip = order_ref[low + n % count]
            role = 2 * chip + (core_ref[0] if n < count else 1 - core_ref[0])
            if start:
                arrivals[n].wait()

            @pl.when(chip < ROLES // 2)
            def _(n=n, role=role):
                copies = [
                    pltpu.make_async_copy(
                        wide.at[n, :, :COLS],
                        wide_out.at[:, pl.ds(pl.multiple_of(role * COLS, 128), COLS)],
                        sems.at[n, 0],
                    ),
                    pltpu.make_async_copy(
                        wide.at[n, :, COLS:],
                        wide_out.at[:, pl.ds(pl.multiple_of(FF + role * COLS, 128), COLS)],
                        sems.at[n, 1],
                    ),
                    pltpu.make_async_copy(
                        down.at[n],
                        down_out.at[pl.ds(pl.multiple_of(role * PIECE, PIECE), PIECE)],
                        sems.at[n, 2],
                    ),
                ]
                if start:
                    wide[n] = narrow[n, :SHARD].astype(F32)
                    copies[0].start()
                    copies[1].start()
                    for (r, c), (rows, cols) in piece_parts():
                        down[n, rows, cols] = narrow[
                            n, SHARD + r.start : SHARD + r.stop, c
                        ].astype(F32)
                    copies[2].start()
                else:
                    for copy in copies:
                        copy.wait()


def write_grads(core, order, mine, other, low, high, held):
    count = high - low
    return pl.pallas_call(
        functools.partial(write_kernel, low, count, len(held)),
        in_specs=scalars(2) + anywhere(2 * count + len(held)),
        out_specs=anywhere(2),
        out_shape=[
            jax.ShapeDtypeStruct((SHARD, 2 * FF), F32),
            jax.ShapeDtypeStruct((FF // 8, D), F32),
        ],
        scratch_shapes=[
            pltpu.VMEM((2 * count, SHARD + 96, 2 * COLS), BF),
            pltpu.VMEM((2 * count, SHARD, 2 * COLS), F32),
            pltpu.VMEM((2 * count, PIECE, D), F32),
            pltpu.SemaphoreType.DMA((2 * count,)),
            pltpu.SemaphoreType.DMA((2 * count, 3)),
        ],
        input_output_aliases={2 + 2 * count + k: k for k in range(len(held))},
        compiler_params=pltpu.CompilerParams(vmem_limit_bytes=48 << 20),
        cost_estimate=cost(2 * count),
    )(core, order, *mine[low:high], *other[low:high], *held)


def project_kernel(order_ref, gain_ref, w_ref, bias_ref, cos_ref, sin_ref, *refs):
    normed_ref, heads_ref, x_all, sems = refs[8:]
    copies = fetch([(refs[k], x_all.at[k]) for k in range(8)], sems)
    for k in range(8):
        copies[k].wait()
        rows = x_all[k].astype(F32)
        scale = lax.rsqrt(jnp.mean(rows * rows, axis=-1, keepdims=True) + NORM_EPSILON)
        normed = (rows * scale * gain_ref[...]).astype(BF)
        at = order_ref[k]
        normed_ref[at] = normed
        out = jnp.dot(normed, w_ref[...], preferred_element_type=F32) + bias_ref[...]
        for h in range(2):
            u = out[:, HEAD * h : HEAD * (h + 1)]
            u = u * cos_ref[...] + pltpu.roll(u, HEAD // 2, 1) * sin_ref[...]
            heads_ref[at, :, HEAD * h : HEAD * (h + 1)] = u.astype(BF)


def whole(count):
    return [pl.BlockSpec(memory_space=pltpu.VMEM)] * count


def scalars(count):
    return [pl.BlockSpec(memory_space=pltpu.SMEM)] * count


def anywhere(count):
    return [pl.BlockSpec(memory_space=pl.ANY)] * count


def fetch(pairs, sems):
    copies = [
        pltpu.make_async_copy(source, target, sems.at[k]) for k, (source, target) in enumerate(pairs)
    ]
    for copy in copies:
        copy.start()
    return copies


def rows_of(ref, k):
    return ref.at[ROWS * k : ROWS * (k + 1)]


def project(order, gain, weight, bias, cosine, signed, blocks):
    return pl.pallas_call(
        project_kernel,
        in_specs=scalars(1) + whole(5) + anywhere(8),
        out_specs=whole(2),
        out_shape=[
            jax.ShapeDtypeStruct((8, ROWS, D), BF),
            jax.ShapeDtypeStruct((8, ROWS, 256), BF),
        ],
        scratch_shapes=[pltpu.VMEM((8, ROWS, D), BF), pltpu.SemaphoreType.DMA((8,))],
        compiler_params=pltpu.CompilerParams(vmem_limit_bytes=32 << 20),
        cost_estimate=cost(4),
    )(order, gain, weight, bias, cosine, signed, *blocks)


def head_stack(ref, side):
    return jnp.concatenate(
        [
            ref[h // 2, :, HEAD * (h % 2) : HEAD * (h % 2 + 1)]
            for h in range(GROUPS * side, GROUPS * (side + 1))
        ],
        axis=0,
    )


def scores_of(me_ref, queries, keys):
    raw = lax.dot_general(
        queries, keys, (((1,), (1,)), ((), ())), preferred_element_type=F32
    )
    raw = raw.reshape(GROUPS, ROWS, 8 * ROWS) * HEAD ** (-0.5)
    row = me_ref[0] * ROWS + lax.broadcasted_iota(jnp.int32, (ROWS, 8 * ROWS), 0)
    col = lax.broadcasted_iota(jnp.int32, (ROWS, 8 * ROWS), 1)
    return jnp.where((col <= row)[None], raw, -1e30)


def attend_kernel(me_ref, heads_ref, kv_ref, out_ref, log_ref):
    kv = kv_ref[...].reshape(8 * ROWS, 512)
    for side in range(2):
        keys = kv[:, HEAD * side : HEAD * (side + 1)]
        values = kv[:, 256 + HEAD * side : 256 + HEAD * (side + 1)]
        scores = scores_of(me_ref, head_stack(heads_ref, side), keys)
        top = jnp.max(scores, axis=-1, keepdims=True)
        exponent = jnp.exp(scores - top)
        row_total = jnp.sum(exponent, axis=-1, keepdims=True)
        mixed = jnp.dot(
            exponent.astype(BF).reshape(GROUPS * ROWS, 8 * ROWS),
            values,
            preferred_element_type=F32,
        ).reshape(GROUPS, ROWS, HEAD)
        mixed = mixed / row_total
        logs = top + jnp.log(row_total)
        for i in range(GROUPS):
            h = GROUPS * side + i
            out_ref[:, HEAD * h : HEAD * (h + 1)] = mixed[i].astype(BF)
            log_ref[h] = logs[i]


def attend(me, heads, kv):
    return pl.pallas_call(
        attend_kernel,
        in_specs=[pl.BlockSpec(memory_space=pltpu.SMEM)] + whole(2),
        out_specs=whole(2),
        out_shape=[
            jax.ShapeDtypeStruct((ROWS, WIDTH_Q), BF),
            jax.ShapeDtypeStruct((HEADS, ROWS, 1), F32),
        ],
        compiler_params=pltpu.CompilerParams(vmem_limit_bytes=48 << 20),
        cost_estimate=cost(5),
    )(me, heads, kv)


def attend_back_kernel(
    me_ref, heads_ref, kv_ref, grad_ref, log_ref, cos_ref, sin_ref, dq_ref, dkv_ref
):
    kv = kv_ref[...].reshape(8 * ROWS, 512)
    for side in range(2):
        keys = kv[:, HEAD * side : HEAD * (side + 1)]
        values = kv[:, 256 + HEAD * side : 256 + HEAD * (side + 1)]
        queries = head_stack(heads_ref, side)
        grads = jnp.concatenate(
            [
                grad_ref[:, HEAD * h : HEAD * (h + 1)]
                for h in range(GROUPS * side, GROUPS * (side + 1))
            ],
            axis=0,
        )
        scores = scores_of(me_ref, queries, keys)
        probs = jnp.exp(scores - log_ref[GROUPS * side : GROUPS * (side + 1)])
        grad_probs = contract_cols(grads, values).reshape(GROUPS, ROWS, 8 * ROWS)
        inner = jnp.sum(probs * grad_probs, axis=-1, keepdims=True)
        grad_scores = (probs * (grad_probs - inner)).astype(BF)
        grad_scores = grad_scores.reshape(GROUPS * ROWS, 8 * ROWS)
        probs_low = probs.astype(BF).reshape(GROUPS * ROWS, 8 * ROWS)
        dq = jnp.dot(grad_scores, keys, preferred_element_type=F32) * HEAD ** (-0.5)
        dk = contract_rows(grad_scores, queries) * HEAD ** (-0.5)
        dv = contract_rows(probs_low, grads)
        for i in range(GROUPS):
            h = GROUPS * side + i
            u = dq[ROWS * i : ROWS * (i + 1)]
            u = u * cos_ref[...] - pltpu.roll(u, HEAD // 2, 1) * sin_ref[...]
            dq_ref[:, HEAD * h : HEAD * (h + 1)] = u.astype(BF)
        low, high = HEAD * side, HEAD * (side + 1)
        dkv_ref[:, :, low:high] = dk.astype(BF).reshape(8, ROWS, HEAD)
        dkv_ref[:, :, 256 + low : 256 + high] = dv.astype(BF).reshape(8, ROWS, HEAD)


def attend_back(me, heads, kv, grads, logs, cosine, signed):
    return pl.pallas_call(
        attend_back_kernel,
        in_specs=[pl.BlockSpec(memory_space=pltpu.SMEM)] + whole(6),
        out_specs=whole(2),
        out_shape=[
            jax.ShapeDtypeStruct((ROWS, WIDTH_Q), BF),
            jax.ShapeDtypeStruct((8, ROWS, 512), BF),
        ],
        compiler_params=pltpu.CompilerParams(vmem_limit_bytes=56 << 20),
        cost_estimate=cost(9),
    )(me, heads, kv, grads, logs, cosine, signed)


def halves(core_ref, mine, other):
    first = core_ref[0] == 0
    return jnp.where(first, mine, other), jnp.where(first, other, mine)


def middle_kernel(
    core_ref, att_ref, x_ref, gain_ref, mine_ref, other_ref, mid_ref, scale_ref, h_ref
):
    att = att_ref[...]
    mine = jnp.dot(att, mine_ref[...], preferred_element_type=F32)
    other = jnp.dot(att, other_ref[...], preferred_element_type=F32)
    low, high = halves(core_ref, mine, other)
    low = x_ref[:, : D // 2].astype(F32) + low
    high = x_ref[:, D // 2 :].astype(F32) + high
    square = jnp.sum(low * low, axis=-1, keepdims=True) + jnp.sum(
        high * high, axis=-1, keepdims=True
    )
    scale = lax.rsqrt(square / D + NORM_EPSILON)
    scale_ref[...] = scale
    mid_ref[:, : D // 2] = low
    mid_ref[:, D // 2 :] = high
    h_ref[:, : D // 2] = (low * scale * gain_ref[:, : D // 2]).astype(BF)
    h_ref[:, D // 2 :] = (high * scale * gain_ref[:, D // 2 :]).astype(BF)


def middle_of(core, attended, rows, gain, mine, other):
    return pl.pallas_call(
        middle_kernel,
        in_specs=[pl.BlockSpec(memory_space=pltpu.SMEM)]
        + whole(5),
        out_specs=whole(3),
        out_shape=[
            jax.ShapeDtypeStruct((ROWS, D), F32),
            jax.ShapeDtypeStruct((ROWS, 1), F32),
            jax.ShapeDtypeStruct((ROWS, D), BF),
        ],
        compiler_params=pltpu.CompilerParams(vmem_limit_bytes=24 << 20),
        cost_estimate=cost(3),
    )(core, attended, rows, gain, mine, other)


def turning_kernel(core_ref, mid_ref, scale_ref, gain_ref, cot_ref, mine_ref, other_ref, *refs):
    mid_grad_ref, branch_ref, att_ref, gain_grad_ref, arrived, sems = refs[5:]
    copies = fetch([(refs[k], arrived.at[k]) for k in range(5)], sems)
    for copy in copies:
        copy.wait()
    grad = arrived[0].astype(F32)
    for k in range(1, 5):
        grad = grad + arrived[k].astype(F32)
    mid, scale = mid_ref[...], scale_ref[...]
    gain_grad_ref[...] = jnp.sum(grad * mid * scale, axis=0, keepdims=True)
    weighted = grad * gain_ref[...]
    mean = jnp.mean(weighted * mid, axis=-1, keepdims=True)
    grad = cot_ref[...].astype(F32) + scale * (weighted - mid * (scale * scale * mean))
    mid_grad_ref[...] = grad
    branch = grad.astype(BF)
    branch_ref[...] = branch
    mine, other = halves(core_ref, branch[:, : D // 2], branch[:, D // 2 :])
    att = contract_cols(mine, mine_ref[...]) + contract_cols(other, other_ref[...])
    att_ref[...] = att.astype(BF)


def turning(core, middle, scale, gain, cotangent, mine, other, parts):
    return pl.pallas_call(
        turning_kernel,
        in_specs=[pl.BlockSpec(memory_space=pltpu.SMEM)]
        + whole(6)
        + anywhere(5),
        out_specs=whole(4),
        out_shape=[
            jax.ShapeDtypeStruct((ROWS, D), F32),
            jax.ShapeDtypeStruct((ROWS, D), BF),
            jax.ShapeDtypeStruct((ROWS, D), BF),
            jax.ShapeDtypeStruct((1, D), F32),
        ],
        scratch_shapes=[pltpu.VMEM((5, ROWS, D), BF), pltpu.SemaphoreType.DMA((5,))],
        compiler_params=pltpu.CompilerParams(vmem_limit_bytes=32 << 20),
        cost_estimate=cost(4.2),
    )(core, middle, scale, gain, cotangent, mine, other, *parts)


def feed_kernel(held, order_ref, *refs):
    h_refs, c_ref, weights = refs[:4], refs[4], refs[5:7]
    up_w, packed, down_w, h_all, c_all, total_ref, rows_ref, sems, row_sems, in_sems = refs[-10:]
    outs = refs[7 + held : -10]
    act_refs, grad_refs, out_ref, part_refs = outs[:2], outs[2:4], outs[4], outs[5:]
    first = 4 if held else 0
    copies = []
    for side in range(2):
        for n, (rows, target) in enumerate(
            ((slice(0, SHARD), up_w), (slice(SHARD, SHARD + 96), packed))
        ):
            copy = pltpu.make_async_copy(
                weights[side].at[:, rows], target.at[side], sems.at[side, n]
            )
            copy.start()
            copies.append(copy)
    tokens = fetch(
        [(h_refs[i], rows_of(h_all, i)) for i in range(4)]
        + [(c_ref.at[order_ref[first + i]], rows_of(c_all, i)) for i in range(4)],
        in_sems,
    )
    for copy in tokens:
        copy.wait()
    for side in range(2):
        grad_ref = grad_refs[side]
        copies[2 * side].wait()
        up_now = up_w[side].reshape(D, 2 * COLS)
        gate_up = jnp.dot(h_all[...], up_now, preferred_element_type=F32)
        copies[2 * side + 1].wait()
        for g in range(8):
            for (r, c), (rows, cols) in piece_parts():
                down_w[PIECE * g + rows.start : PIECE * g + rows.stop, cols] = packed[side, g, r, c]
        grad_act = contract_cols(c_all[...], down_w[...])
        gate, up = gate_up[:, :COLS], gate_up[:, COLS:]
        sig = jax.nn.sigmoid(gate)
        silu = gate * sig
        act_refs[side][...] = (silu * up).astype(BF)
        rows = jnp.dot(act_refs[side][...], down_w[...], preferred_element_type=F32)
        grad_ref[:, :COLS] = (grad_act * up * sig * (1.0 + gate * (1.0 - sig))).astype(BF)
        grad_ref[:, COLS:] = (grad_act * silu).astype(BF)
        if side == 0:
            total_ref[...] = rows
            part = contract_cols(grad_ref[...], up_now)
        else:
            rows_ref[...] = (total_ref[...] + rows).astype(BF)
            copies = []
            for i in range(4):
                copy = pltpu.make_async_copy(
                    rows_ref.at[ROWS * i : ROWS * (i + 1)],
                    out_ref.at[order_ref[first + i]],
                    row_sems.at[i],
                )
                copy.start()
                copies.append(copy)
            part = part + contract_cols(grad_ref[...], up_now)
            for i in range(4):
                part_refs[i][...] = part[ROWS * i : ROWS * (i + 1)].astype(BF)
            for copy in copies:
                copy.wait()


def feed(order, h_blocks, cot_all, mine, other, held):
    tokens = 4 * ROWS
    at = 1 if held else 0
    widths = (COLS, COLS, 2 * COLS, 2 * COLS)
    outs = pl.pallas_call(
        functools.partial(feed_kernel, len(held)),
        grid=(1,),
        in_specs=scalars(1) + anywhere(7 + len(held)),
        out_specs=[pl.BlockSpec((tokens, w), lambda i: (at, 0)) for w in widths]
        + anywhere(1)
        + whole(4),
        out_shape=[jax.ShapeDtypeStruct((2 * tokens, w), BF) for w in widths]
        + [jax.ShapeDtypeStruct((8, ROWS, D), BF)]
        + [jax.ShapeDtypeStruct((ROWS, D), BF)] * 4,
        scratch_shapes=[
            pltpu.VMEM((2, 8, SHARD, 2 * COLS), BF),
            pltpu.VMEM((2, 8, 96, 2 * COLS), BF),
            pltpu.VMEM((COLS, D), BF),
            pltpu.VMEM((tokens, D), BF),
            pltpu.VMEM((tokens, D), BF),
            pltpu.VMEM((tokens, D), F32),
            pltpu.VMEM((tokens, D), BF),
            pltpu.SemaphoreType.DMA((2, 2)),
            pltpu.SemaphoreType.DMA((4,)),
            pltpu.SemaphoreType.DMA((8,)),
        ],
        input_output_aliases={8 + k: k for k in range(len(held))},
        compiler_params=pltpu.CompilerParams(vmem_limit_bytes=56 << 20),
        cost_estimate=cost(21),
    )(order, *h_blocks, cot_all, mine, other, *held)
    return tuple(outs[:5]), outs[5:]


def assemble_kernel(dq_ref, dkv_ref, branch_ref, cos_ref, sin_ref, both_ref, out_ref):
    dkv = dkv_ref[0].astype(F32)
    for k in range(1, 8):
        dkv = dkv + dkv_ref[k].astype(F32)
    for h in range(2):
        u = dkv[:, HEAD * h : HEAD * (h + 1)]
        u = u * cos_ref[...] - pltpu.roll(u, HEAD // 2, 1) * sin_ref[...]
        u = u.astype(BF)
        both_ref[6, :, HEAD * h : HEAD * (h + 1)] = u
        out_ref[:, WIDTH_Q + HEAD * h : WIDTH_Q + HEAD * (h + 1)] = u
    u = dkv[:, 256:].astype(BF)
    both_ref[7, :, :256] = u
    out_ref[:, WIDTH_Q + 256 :] = u
    for q in range(6):
        u = dq_ref[:, 256 * q : 256 * (q + 1)]
        both_ref[q, :, :256] = u
        out_ref[:, 256 * q : 256 * (q + 1)] = u
        both_ref[q, :, 256:] = branch_ref[:, 256 * q : 256 * (q + 1)]
    for q in range(6, 8):
        both_ref[q, :, 256:] = jnp.zeros((ROWS, 256), BF)


def assemble(dq, dkv, branch, cosine, signed):
    return pl.pallas_call(
        assemble_kernel,
        in_specs=whole(5),
        out_specs=whole(2),
        out_shape=[
            jax.ShapeDtypeStruct((8, ROWS, 512), BF),
            jax.ShapeDtypeStruct((ROWS, QKV), BF),
        ],
        compiler_params=pltpu.CompilerParams(vmem_limit_bytes=16 << 20),
        cost_estimate=cost(1.2),
    )(dq, dkv, branch, cosine, signed)


def on_device(hidden_in, norm_attn, w_qkv, b_qkv, w_out, norm_mlp, w_gate_up, w_down, cotangent):
    core = lax.axis_index("c")
    plane = lax.axis_index(PLANE)
    replica = lax.axis_index(REPLICA)
    group = lax.axis_index(GROUP)
    yl, zz = lax.axis_index("yl"), lax.axis_index("z")
    yh, xx = lax.axis_index("yh"), lax.axis_index("x")
    first_row = group * ROWS
    works = replica < ROLES
    role = jnp.minimum(replica, ROLES - 1)

    x_blocks = send_out(hidden_in[0], PLANE)
    pad = jnp.zeros((64,), BF)
    small = jnp.concatenate([b_qkv, norm_attn, pad, norm_mlp, pad]).reshape(3, 256)
    columns = lax.dynamic_slice(w_qkv, (0, plane * 256), (SHARD, 256))
    columns = jnp.concatenate([columns, small, jnp.zeros((13, 256), BF)], axis=0)
    columns = gather_direct(after(columns, *x_blocks[1:5]), GROUP)
    columns = after(columns, *x_blocks[5:])
    qkv_role = columns[:, :SHARD].reshape(D, 256)
    bias_full = columns[:, SHARD : SHARD + 1].astype(F32)
    gain_one = columns[:, SHARD + 1, :SHARD].reshape(1, D).astype(F32)
    gain_two = columns[:, SHARD + 2, :SHARD].reshape(1, D).astype(F32)

    out_half = lax.dynamic_slice(w_out, (0, core * 768), (SHARD, 768))
    out_mine = lax.all_gather(out_half, GROUP, axis=0, tiled=True)
    piece = lax.dynamic_slice(w_down, (role * PIECE, 0), (PIECE, D))
    piece = lax.ppermute(piece, EVERY, down_pairs())
    (packed,) = call(
        pack_kernel,
        1,
        [((SHARD + 96, 2 * COLS), BF)],
        scalars(1) + whole(3),
        works.astype(jnp.int32).reshape(1),
        lax.dynamic_slice(w_gate_up, (0, role * COLS), (SHARD, COLS)),
        lax.dynamic_slice(w_gate_up, (0, FF + role * COLS), (SHARD, COLS)),
        piece,
    )
    feed_mine = lax.all_gather(after(packed, x_blocks[1]), GROUP, axis=0)

    cosine, signed = rope_tables(first_row, ROWS, HEAD)
    turns = plane < 7
    order = jnp.stack([place(yl, zz, o, -1) for o in ALL_OFFSETS]).astype(jnp.int32)
    normed_one_all, heads = project(
        order,
        gain_one,
        qkv_role,
        pick(bias_full, plane),
        jnp.where(turns, cosine, 1.0),
        jnp.where(turns, signed, 0.0),
        x_blocks,
    )

    heads = lax.all_to_all(heads, PLANE, 0, 0, tiled=True)
    out_other = swap(after(out_mine, heads))
    grad_out = cotangent[0]
    cot_blocks = send_out(after(grad_out, *x_blocks), PLANE)
    kv_own = jnp.concatenate([heads[6], heads[7]], axis=1)
    kv_own = after(kv_own, *cot_blocks[1:5])
    kv_all = gather_direct(kv_own, GROUP)
    kv_all = after(kv_all, *cot_blocks)
    cot_all = arrange(order, cot_blocks)
    me = group.astype(jnp.int32).reshape(1)
    attended, logs = attend(me, heads, kv_all)
    which = core.astype(jnp.int32).reshape(1)
    middle, scale_two, normed_two = middle_of(
        which, attended, hidden_in[0], gain_two, out_mine, out_other
    )

    h_blocks = send_out(normed_two, PLANE)
    feed_other = swap(after(feed_mine, *h_blocks[1:3]))
    attended_all = lax.all_gather(after(attended, *h_blocks[1:5]), PLANE, axis=0)
    qkv_half = lax.dynamic_slice(w_qkv, (0, core * 1024), (SHARD, 1024))
    qkv_mine = lax.all_gather(after(qkv_half, *h_blocks[1:5]), GROUP, axis=0, tiled=True)
    held, back_blocks = (), {}
    for part in (slice(0, 4), slice(4, 8)):
        held, parts = feed(order, h_blocks[part], cot_all, feed_mine, feed_other, held)
        for o, block in zip(ALL_OFFSETS[part], parts):
            back_blocks[back(o)] = block
    second_parts, _, round_sums = send_parts(back_blocks, PLANE)

    held_h = after(tuple(h_blocks), parts, attended_all)
    given = weight_grads(order, held_h, cot_all, held[3], held[1])
    group_order = jnp.stack([place(yh, xx, o) for o in ALL_OFFSETS]).astype(jnp.int32)
    merged = merged_grads(
        order, group_order, after(held_h, qkv_mine), cot_all, held[2], held[0], swap(given)
    )
    second_parts = after(second_parts, merged)
    grad_middle, grad_branch, grad_attended, gain_two_grad = turning(
        which, middle, scale_two, gain_two, grad_out, out_mine, out_other, second_parts
    )
    grad_q, grad_kv = attend_back(me, heads, kv_all, grad_attended, logs, cosine, signed)
    mlp_parts, mlp_first, _ = send_parts(
        dict(zip(ALL_OFFSETS, merged)), GROUP
    )
    grad_kv = after(grad_kv, *mlp_first)
    grad_kv = lax.all_to_all(grad_kv, GROUP, 0, 0, tiled=True)

    out_rows = after(held[4], *second_parts).reshape(8 * ROWS, D)
    out_rows = lax.psum_scatter(out_rows, PLANE, scatter_dimension=0, tiled=True)
    result = (middle + out_rows.astype(F32)).astype(BF)[None]
    grad_kv = after(grad_kv, out_rows)

    both, grad_projected = assemble(grad_q, grad_kv, grad_branch, cosine, signed)
    qkv_other = swap(after(qkv_mine, both))
    assembled = both
    both = lax.all_to_all(both, PLANE, 0, 0, tiled=True)

    mlp_grad = total(after(tuple(mlp_parts), assembled)).astype(BF)
    down_grad = lax.ppermute(mlp_grad[SHARD:], EVERY, [(t, s) for s, t in down_pairs()])
    mlp_grad = jnp.concatenate([mlp_grad[:SHARD], down_grad], axis=0)
    grad_blocks = send_out(mlp_grad, PLANE)
    other_blocks = [swap(b) for b in grad_blocks]
    feed_grads = write_grads(which, order, grad_blocks, other_blocks, 0, 5, ())
    gate_up_grad, down_grad = write_grads(which, order, grad_blocks, other_blocks, 5, 8, feed_grads)

    grad_in, gain_one_grad = finish(
        which, grad_projected, qkv_mine, qkv_other, hidden_in[0], gain_one, grad_middle
    )
    gains = jnp.stack([gain_one_grad[0], gain_two_grad[0]]).astype(BF).reshape(2, 8, SHARD)
    gains = jnp.pad(gains.transpose(1, 0, 2), ((0, 0), (0, 14), (0, 64)))
    keep, give, bias_grad = attention_grads(which, normed_one_all, attended_all, both)
    (payload,) = call(
        payload_kernel, 1.4,
        [((8, SHARD + 16, 256), BF)],
        whole(4),
        keep,
        swap(give),
        gains,
        bias_grad,
    )
    payload = lax.all_to_all(payload, GROUP, 0, 0, tiled=True)
    (payload,) = call(sum_kernel, 1, [((8, SHARD + 16, 256), BF)], whole(1), payload)
    mine = lax.all_to_all(payload, PLANE, 0, 0, tiled=True)
    mine = after(mine, *feed_grads)
    other = swap(mine)
    qkv_grad, out_grad, gains, bias_grad = call(
        last_kernel,
        3,
        [((SHARD, QKV), F32), ((SHARD, D), F32), ((16, 256), F32), ((16, 256), F32)],
        [pl.BlockSpec(memory_space=pltpu.SMEM)] * 2 + whole(2),
        which,
        me,
        mine,
        other,
    )

    return (
        result,
        grad_in[None],
        gains[0, :SHARD],
        qkv_grad,
        bias_grad[2],
        out_grad,
        gains[1, :SHARD],
        gate_up_grad,
        down_grad,
    )


def solution(mesh):
    fine = Mesh(mesh.devices.reshape(2, 4, 2, 4, 2), EVERY)
    tokens = P(REPLICA, GROUP, None)
    matrix = P(GROUP, None)
    vector = P(GROUP)
    return jax.shard_map(
        on_device,
        mesh=fine,
        in_specs=(tokens, vector, matrix, vector, matrix, vector, matrix, matrix, tokens),
        out_specs=(tokens, tokens, vector, matrix, vector, matrix, vector, matrix, matrix),
        check_vma=False,
    )
```

```python
import functools

import jax
import jax.numpy as jnp
from jax import lax
from jax.experimental import pallas as pl
from jax.experimental.pallas import tpu as pltpu
from jax.sharding import Mesh, PartitionSpec as P

D = 1536
HEADS = 12
KV_HEADS = 2
HEAD = 128
FF = 8960
QKV = 2048
ROWS = 128
GROUPS = HEADS // KV_HEADS
WIDTH_Q = HEADS * HEAD
WIDTH_K = KV_HEADS * HEAD
ROLES = 14
COLS = FF // ROLES
SHARD = D // 8
PIECE = COLS // 8
PIECES = FF // 8 // PIECE

NORM_EPSILON = 1e-06
ROPE_BASE = 1000000.0
BF = jnp.bfloat16


def cost(micros):
    return pl.CostEstimate(flops=int(micros * SCALE), bytes_accessed=1000, transcendentals=0)


SCALE = 0.58e9
F32 = jnp.float32

GROUP = ("yh", "x")
PLANE = ("yl", "z")
REPLICA = ("yl", "z", "c")
GROUP_CORE = ("yh", "x", "c")
EVERY = ("yh", "x", "yl", "z", "c")

ALL_OFFSETS = ((0, 0), (0, 1), (0, 3), (1, 0), (0, 2), (1, 1), (1, 3), (1, 2))


def shift_pairs(offset):
    dy, dx = offset
    return [
        (y * 4 + x, ((y + dy) % 2) * 4 + (x + dx) % 4) for y in range(2) for x in range(4)
    ]


def back(offset):
    return (offset[0], (4 - offset[1]) % 4)


def send(block, axes, offset):
    return lax.ppermute(block, axes, shift_pairs(offset))


def send_out(block, axes, row=False, hold=()):
    one, three = send(block, axes, (0, 1)), send(block, axes, (0, 3))
    across, two = send(block, axes, (1, 0)), send(block, axes, (0, 2))
    across, two = after((across, two), *hold)
    return [
        block,
        one,
        three,
        across,
        two,
        send(across, axes, (0, 1)),
        send(across, axes, (0, 3)),
        send(across, axes, (0, 2)) if row else send(two, axes, (1, 0)),
    ]


def send_parts(blocks, axes, hold=()):
    first = (
        send(blocks[1, 1], axes, (0, 1)),
        send(blocks[1, 3], axes, (0, 3)),
        send(blocks[1, 2], axes, (1, 0)),
    )
    from_one, from_three, from_across = after(first, *hold)
    two = (blocks[0, 2].astype(F32) + from_across.astype(F32)).astype(BF)
    across = total([blocks[1, 0], from_one, from_three]).astype(BF)
    parts = [
        blocks[0, 0],
        send(blocks[0, 1], axes, (0, 1)),
        send(blocks[0, 3], axes, (0, 3)),
        send(two, axes, (0, 2)),
        send(across, axes, (1, 0)),
    ]
    return parts, first, (two, across)


def after(value, *done):
    return lax.optimization_barrier((value,) + done)[0] if done else value


def total(blocks):
    out = blocks[0].astype(F32)
    for b in blocks[1:]:
        out = out + b.astype(F32)
    return out


def down_pairs():
    pairs = []
    for r in range(ROLES):
        for g in range(8):
            piece = 8 * r + g
            pairs.append(((piece // PIECES) * 16 + piece % PIECES, g * 16 + r))
    return pairs


def rope_tables(first_row, row_count, head_size):
    half_width = head_size // 2
    position = (first_row + jnp.arange(row_count, dtype=jnp.int32)).astype(F32)
    frequency = jnp.power(
        ROPE_BASE, -(jnp.arange(half_width, dtype=jnp.int32).astype(F32) * 2.0) / head_size
    )
    angles = position[:, None] * frequency[None, :]
    cosine = jnp.concatenate([jnp.cos(angles), jnp.cos(angles)], axis=-1)
    signed = jnp.concatenate([-jnp.sin(angles), jnp.sin(angles)], axis=-1)
    return (cosine, signed)


def contract_rows(left_side, right_side):
    return lax.dot_general(
        left_side, right_side, (((0,), (0,)), ((), ())), preferred_element_type=F32
    )


def contract_cols(left_side, right_side):
    return lax.dot_general(
        left_side, right_side, (((1,), (1,)), ((), ())), preferred_element_type=F32
    )


def swap(block):
    return lax.ppermute(block, "c", [(0, 1), (1, 0)])


def gather_direct(block, axes):
    return lax.all_to_all(jnp.broadcast_to(block[None], (8,) + block.shape), axes, 0, 0, tiled=True)


def place(y, x, offset, sign=1):
    return ((y + sign * offset[0]) % 2) * 4 + (x + sign * offset[1]) % 4


def pick(blocks, index):
    return lax.dynamic_index_in_dim(blocks, index, 0, keepdims=False)


def piece_parts():
    for i in range(5):
        for j in range(6):
            low, high = max(96 * i, 80 * j), min(96 * (i + 1), 80 * (j + 1))
            if low < high:
                yield (
                    (slice(low - 96 * i, high - 96 * i), slice(256 * i, 256 * (i + 1))),
                    (slice(low - 80 * j, high - 80 * j), slice(256 * j, 256 * (j + 1))),
                )


def call(kernel, micros, out_shape, in_specs, *args, vmem=48, **more):
    return pl.pallas_call(
        kernel,
        in_specs=in_specs,
        out_specs=[pl.BlockSpec(memory_space=pltpu.VMEM)] * len(out_shape),
        out_shape=[jax.ShapeDtypeStruct(shape, kind) for shape, kind in out_shape],
        compiler_params=pltpu.CompilerParams(vmem_limit_bytes=vmem << 20),
        cost_estimate=cost(micros),
        **more,
    )(*args)


def pack_kernel(works_ref, gate_ref, up_ref, piece_ref, out_ref):
    works = works_ref[0] > 0
    gate, up = gate_ref[...], up_ref[...]
    out_ref[:SHARD, :COLS] = jnp.where(works, gate, jnp.zeros_like(gate))
    out_ref[:SHARD, COLS:] = jnp.where(works, up, jnp.zeros_like(up))
    for (r, c), (rows, cols) in piece_parts():
        out_ref[SHARD + r.start : SHARD + r.stop, c] = piece_ref[rows, cols]


def arrange_kernel(order_ref, *refs):
    for k in range(8):
        refs[8][order_ref[k]] = refs[k][...]


def arrange(order, blocks):
    return call(
        arrange_kernel,
        2,
        [((8,) + blocks[0].shape, BF)],
        [pl.BlockSpec(memory_space=pltpu.SMEM)] + whole(8),
        order,
        *blocks,
    )[0]


def packed_grads(order_ref, refs, up_sum, down_sum, scratch):
    h_all, c_all, grad, act, sems = scratch
    c_ref, grad_ref, act_ref = refs[8:11]
    copies = fetch(
        [(grad_ref, grad)]
        + [(refs[k].at[:ROWS], rows_of(h_all, k)) for k in range(8)]
        + [(act_ref, act)]
        + [(c_ref.at[order_ref[k]], rows_of(c_all, k)) for k in range(8)],
        sems,
    )
    for copy in copies[:9]:
        copy.wait()
    up_sum[...] = contract_rows(h_all[...], grad[...]).reshape(8, SHARD, 2 * COLS).astype(BF)
    for copy in copies[9:]:
        copy.wait()
    down_sum[...] = contract_rows(act[...], c_all[...]).astype(BF)


GRAD_SCRATCH = [
    pltpu.VMEM((8 * ROWS, D), BF),
    pltpu.VMEM((8 * ROWS, D), BF),
    pltpu.VMEM((8 * ROWS, 2 * COLS), BF),
    pltpu.VMEM((8 * ROWS, COLS), BF),
    pltpu.SemaphoreType.DMA((18,)),
]


def weight_kernel(order_ref, *refs):
    out_ref, down_sum = refs[11:13]
    packed_grads(order_ref, refs, out_ref.at[:, :SHARD], down_sum, refs[13:])
    for g in range(8):
        for (r, c), (rows, cols) in piece_parts():
            out_ref[g, SHARD + r.start : SHARD + r.stop, c] = down_sum[
                PIECE * g + rows.start : PIECE * g + rows.stop, cols
            ]


def weight_grads(order, h_blocks, cot_all, grads, acts):
    return call(
        weight_kernel,
        10.7,
        [((8, SHARD + 96, 2 * COLS), BF)],
        scalars(1) + anywhere(11),
        order,
        *h_blocks,
        cot_all,
        grads,
        acts,
        scratch_shapes=[pltpu.VMEM((COLS, D), BF)] + GRAD_SCRATCH,
    )[0]


def merge_kernel(token_order_ref, order_ref, *refs):
    given_ref, outs, (up_sum, down_sum, given, sem) = refs[11], refs[12:20], refs[20:24]
    copy = fetch([(given_ref, given)], sem)[0]
    packed_grads(token_order_ref, refs, up_sum, down_sum, refs[24:])
    copy.wait()
    for k in range(8):
        g = order_ref[k]
        outs[k][:SHARD] = (up_sum[g].astype(F32) + given[g, :SHARD].astype(F32)).astype(BF)
        first = pl.multiple_of(g * PIECE, PIECE)
        for (r, c), (rows, cols) in piece_parts():
            to = slice(SHARD + r.start, SHARD + r.stop)
            own = down_sum[pl.ds(first + rows.start, rows.stop - rows.start), cols]
            outs[k][to, c] = (own.astype(F32) + given[g, to, c].astype(F32)).astype(BF)


def merged_grads(token_order, order, h_blocks, cot_all, grads, acts, given):
    return call(
        merge_kernel,
        15,
        [((SHARD + 96, 2 * COLS), BF)] * 8,
        scalars(2) + anywhere(12),
        token_order,
        order,
        *h_blocks,
        cot_all,
        grads,
        acts,
        given,
        vmem=56,
        scratch_shapes=[
            pltpu.VMEM((8, SHARD, 2 * COLS), BF),
            pltpu.VMEM((COLS, D), BF),
            pltpu.VMEM((8, SHARD + 96, 2 * COLS), BF),
            pltpu.SemaphoreType.DMA((1,)),
        ]
        + GRAD_SCRATCH,
    )


def finish_kernel(
    core_ref, grad_ref, mine_ref, other_ref, x_ref, gain_ref, mid_ref, out_ref, gain_grad_ref
):
    half = QKV // 2
    grad = grad_ref[...]
    mine, other = halves(core_ref, grad[:, :half], grad[:, half:])
    normed = contract_cols(mine, mine_ref[...]) + contract_cols(other, other_ref[...])
    x = x_ref[...].astype(F32)
    scale = lax.rsqrt(jnp.mean(x * x, axis=-1, keepdims=True) + NORM_EPSILON)
    gain_grad_ref[...] = jnp.sum(normed * x * scale, axis=0, keepdims=True)
    weighted = normed * gain_ref[...]
    mean = jnp.mean(weighted * x, axis=-1, keepdims=True)
    out_ref[...] = mid_ref[...] + scale * (weighted - x * (scale * scale * mean))


def finish(core, grad_projected, mine, other, rows, gain, grad_middle):
    return call(
        finish_kernel, 5,
        [((ROWS, D), F32), ((1, D), F32)],
        [pl.BlockSpec(memory_space=pltpu.SMEM)] + whole(6),
        core,
        grad_projected,
        mine,
        other,
        rows,
        gain,
        grad_middle,
    )


def attention_grads_kernel(core_ref, order_ref, normed_ref, both_ref, *refs):
    keep_ref, give_ref, bias_ref, att_all, sems = refs[8:]
    copies = fetch(
        [(refs[k].at[ROWS:], att_all.at[order_ref[k]]) for k in range(8)], sems
    )
    both = both_ref[...].reshape(8 * ROWS, 512)
    role = both[:, :256]
    bias_ref[...] = jnp.sum(role.astype(F32), axis=0, keepdims=True)
    qkv = contract_rows(normed_ref[...].reshape(8 * ROWS, D), role)
    for copy in copies:
        copy.wait()
    out = contract_rows(att_all[...].reshape(8 * ROWS, D), both[:, 256:])
    keep, give = halves(core_ref, qkv, out)
    keep_ref[...] = keep
    give_ref[...] = give.astype(BF)


def attention_grads(core, order, normed, both, bundles):
    return call(
        attention_grads_kernel,
        5,
        [((D, 256), F32), ((D, 256), BF), ((1, 256), F32)],
        scalars(2) + whole(2) + anywhere(8),
        core,
        order,
        normed,
        both,
        *bundles,
        scratch_shapes=[pltpu.VMEM((8, ROWS, D), BF), pltpu.SemaphoreType.DMA((8,))],
    )


def last_kernel(core_ref, group_ref, mine_ref, other_ref, qkv_ref, out_ref, gain_ref, bias_ref):
    gains = jnp.zeros((16, 256), F32)
    for q in range(8):
        mine, other = mine_ref[q].astype(F32), other_ref[q].astype(F32)
        qkv, out = halves(core_ref, mine[:SHARD], other[:SHARD])
        qkv_ref[:, 256 * q : 256 * (q + 1)] = qkv
        if q < 6:
            out_ref[:, 256 * q : 256 * (q + 1)] = out
        gains = gains + mine[SHARD:] + other[SHARD:]
    gain_ref[...] = gains
    g = group_ref[0]
    bias_ref[...] = mine_ref[g, SHARD:].astype(F32) + other_ref[g, SHARD:].astype(F32)


def payload_kernel(keep_ref, other_ref, extra_ref, bias_ref, out_ref):
    row = lax.broadcasted_iota(jnp.int32, (16, 256), 0)
    bias = bias_ref[...].astype(BF).astype(F32)
    for g in range(8):
        rows = slice(SHARD * g, SHARD * (g + 1))
        out_ref[g, :SHARD] = (keep_ref[rows] + other_ref[rows].astype(F32)).astype(BF)
        extra = extra_ref[g].astype(F32)
        out_ref[g, SHARD:] = jnp.where(row == 2, bias, extra).astype(BF)


def sum_kernel(in_ref, out_ref):
    rows = in_ref[0].astype(F32)
    for g in range(1, 8):
        rows = rows + in_ref[g].astype(F32)
    rows = rows.astype(BF)
    for g in range(8):
        out_ref[g] = rows


def write_kernel(low, count, held, core_ref, order_ref, *refs):
    blocks = refs[: 2 * count]
    wide_out, down_out, narrow, wide, down, in_sems, sems = refs[2 * count + held :]
    arrivals = fetch([(blocks[n], narrow.at[n]) for n in range(2 * count)], in_sems)
    for start in (True, False):
        for n in range(2 * count):
            chip = order_ref[low + n % count]
            role = 2 * chip + (core_ref[0] if n < count else 1 - core_ref[0])
            if start:
                arrivals[n].wait()

            @pl.when(chip < ROLES // 2)
            def _(n=n, role=role):
                copies = [
                    pltpu.make_async_copy(
                        wide.at[n, :, :COLS],
                        wide_out.at[:, pl.ds(pl.multiple_of(role * COLS, 128), COLS)],
                        sems.at[n, 0],
                    ),
                    pltpu.make_async_copy(
                        wide.at[n, :, COLS:],
                        wide_out.at[:, pl.ds(pl.multiple_of(FF + role * COLS, 128), COLS)],
                        sems.at[n, 1],
                    ),
                    pltpu.make_async_copy(
                        down.at[n],
                        down_out.at[pl.ds(pl.multiple_of(role * PIECE, PIECE), PIECE)],
                        sems.at[n, 2],
                    ),
                ]
                if start:
                    wide[n] = narrow[n, :SHARD].astype(F32)
                    copies[0].start()
                    copies[1].start()
                    for (r, c), (rows, cols) in piece_parts():
                        down[n, rows, cols] = narrow[
                            n, SHARD + r.start : SHARD + r.stop, c
                        ].astype(F32)
                    copies[2].start()
                else:
                    for copy in copies:
                        copy.wait()


def write_grads(core, order, mine, other, low, high, held):
    count = high - low
    return pl.pallas_call(
        functools.partial(write_kernel, low, count, len(held)),
        in_specs=scalars(2) + anywhere(2 * count + len(held)),
        out_specs=anywhere(2),
        out_shape=[
            jax.ShapeDtypeStruct((SHARD, 2 * FF), F32),
            jax.ShapeDtypeStruct((FF // 8, D), F32),
        ],
        scratch_shapes=[
            pltpu.VMEM((2 * count, SHARD + 96, 2 * COLS), BF),
            pltpu.VMEM((2 * count, SHARD, 2 * COLS), F32),
            pltpu.VMEM((2 * count, PIECE, D), F32),
            pltpu.SemaphoreType.DMA((2 * count,)),
            pltpu.SemaphoreType.DMA((2 * count, 3)),
        ],
        input_output_aliases={2 + 2 * count + k: k for k in range(len(held))},
        compiler_params=pltpu.CompilerParams(vmem_limit_bytes=48 << 20),
        cost_estimate=cost(2 * count),
    )(core, order, *mine[low:high], *other[low:high], *held)


def project_kernel(order_ref, gain_ref, w_ref, bias_ref, cos_ref, sin_ref, *refs):
    normed_ref, heads_ref, x_all, sems = refs[8:]
    copies = fetch([(refs[k], x_all.at[k]) for k in range(8)], sems)
    for k in range(8):
        copies[k].wait()
        rows = x_all[k].astype(F32)
        scale = lax.rsqrt(jnp.mean(rows * rows, axis=-1, keepdims=True) + NORM_EPSILON)
        normed = (rows * scale * gain_ref[...]).astype(BF)
        at = order_ref[k]
        normed_ref[at] = normed
        out = jnp.dot(normed, w_ref[...], preferred_element_type=F32) + bias_ref[...]
        for h in range(2):
            u = out[:, HEAD * h : HEAD * (h + 1)]
            u = u * cos_ref[...] + pltpu.roll(u, HEAD // 2, 1) * sin_ref[...]
            heads_ref[at, :, HEAD * h : HEAD * (h + 1)] = u.astype(BF)


def whole(count):
    return [pl.BlockSpec(memory_space=pltpu.VMEM)] * count


def scalars(count):
    return [pl.BlockSpec(memory_space=pltpu.SMEM)] * count


def anywhere(count):
    return [pl.BlockSpec(memory_space=pl.ANY)] * count


def fetch(pairs, sems):
    copies = [
        pltpu.make_async_copy(source, target, sems.at[k]) for k, (source, target) in enumerate(pairs)
    ]
    for copy in copies:
        copy.start()
    return copies


def rows_of(ref, k):
    return ref.at[ROWS * k : ROWS * (k + 1)]


def project(order, gain, weight, bias, cosine, signed, blocks):
    return pl.pallas_call(
        project_kernel,
        in_specs=scalars(1) + whole(5) + anywhere(8),
        out_specs=whole(2),
        out_shape=[
            jax.ShapeDtypeStruct((8, ROWS, D), BF),
            jax.ShapeDtypeStruct((8, ROWS, 256), BF),
        ],
        scratch_shapes=[pltpu.VMEM((8, ROWS, D), BF), pltpu.SemaphoreType.DMA((8,))],
        compiler_params=pltpu.CompilerParams(vmem_limit_bytes=32 << 20),
        cost_estimate=cost(4),
    )(order, gain, weight, bias, cosine, signed, *blocks)


def head_stack(ref, side):
    return jnp.concatenate(
        [
            ref[h // 2, :, HEAD * (h % 2) : HEAD * (h % 2 + 1)]
            for h in range(GROUPS * side, GROUPS * (side + 1))
        ],
        axis=0,
    )


def scores_of(me_ref, queries, keys):
    raw = lax.dot_general(
        queries, keys, (((1,), (1,)), ((), ())), preferred_element_type=F32
    )
    raw = raw.reshape(GROUPS, ROWS, 8 * ROWS) * HEAD ** (-0.5)
    row = me_ref[0] * ROWS + lax.broadcasted_iota(jnp.int32, (ROWS, 8 * ROWS), 0)
    col = lax.broadcasted_iota(jnp.int32, (ROWS, 8 * ROWS), 1)
    return jnp.where((col <= row)[None], raw, -1e30)


def attend_kernel(me_ref, heads_ref, kv_ref, out_ref, log_ref):
    kv = kv_ref[...].reshape(8 * ROWS, 512)
    for side in range(2):
        keys = kv[:, HEAD * side : HEAD * (side + 1)]
        values = kv[:, 256 + HEAD * side : 256 + HEAD * (side + 1)]
        scores = scores_of(me_ref, head_stack(heads_ref, side), keys)
        top = jnp.max(scores, axis=-1, keepdims=True)
        exponent = jnp.exp(scores - top)
        row_total = jnp.sum(exponent, axis=-1, keepdims=True)
        mixed = jnp.dot(
            exponent.astype(BF).reshape(GROUPS * ROWS, 8 * ROWS),
            values,
            preferred_element_type=F32,
        ).reshape(GROUPS, ROWS, HEAD)
        mixed = mixed / row_total
        logs = top + jnp.log(row_total)
        for i in range(GROUPS):
            h = GROUPS * side + i
            out_ref[:, HEAD * h : HEAD * (h + 1)] = mixed[i].astype(BF)
            log_ref[h] = logs[i]


def attend(me, heads, kv):
    return pl.pallas_call(
        attend_kernel,
        in_specs=[pl.BlockSpec(memory_space=pltpu.SMEM)] + whole(2),
        out_specs=whole(2),
        out_shape=[
            jax.ShapeDtypeStruct((ROWS, WIDTH_Q), BF),
            jax.ShapeDtypeStruct((HEADS, ROWS, 1), F32),
        ],
        compiler_params=pltpu.CompilerParams(vmem_limit_bytes=48 << 20),
        cost_estimate=cost(5),
    )(me, heads, kv)


def attend_back_kernel(
    me_ref, heads_ref, kv_ref, grad_ref, log_ref, cos_ref, sin_ref, dq_ref, dkv_ref
):
    kv = kv_ref[...].reshape(8 * ROWS, 512)
    for side in range(2):
        keys = kv[:, HEAD * side : HEAD * (side + 1)]
        values = kv[:, 256 + HEAD * side : 256 + HEAD * (side + 1)]
        queries = head_stack(heads_ref, side)
        grads = jnp.concatenate(
            [
                grad_ref[:, HEAD * h : HEAD * (h + 1)]
                for h in range(GROUPS * side, GROUPS * (side + 1))
            ],
            axis=0,
        )
        scores = scores_of(me_ref, queries, keys)
        probs = jnp.exp(scores - log_ref[GROUPS * side : GROUPS * (side + 1)])
        grad_probs = contract_cols(grads, values).reshape(GROUPS, ROWS, 8 * ROWS)
        inner = jnp.sum(probs * grad_probs, axis=-1, keepdims=True)
        grad_scores = (probs * (grad_probs - inner)).astype(BF)
        grad_scores = grad_scores.reshape(GROUPS * ROWS, 8 * ROWS)
        probs_low = probs.astype(BF).reshape(GROUPS * ROWS, 8 * ROWS)
        dq = jnp.dot(grad_scores, keys, preferred_element_type=F32) * HEAD ** (-0.5)
        dk = contract_rows(grad_scores, queries) * HEAD ** (-0.5)
        dv = contract_rows(probs_low, grads)
        for i in range(GROUPS):
            h = GROUPS * side + i
            u = dq[ROWS * i : ROWS * (i + 1)]
            u = u * cos_ref[...] - pltpu.roll(u, HEAD // 2, 1) * sin_ref[...]
            dq_ref[:, HEAD * h : HEAD * (h + 1)] = u.astype(BF)
        low, high = HEAD * side, HEAD * (side + 1)
        dkv_ref[:, :, low:high] = dk.astype(BF).reshape(8, ROWS, HEAD)
        dkv_ref[:, :, 256 + low : 256 + high] = dv.astype(BF).reshape(8, ROWS, HEAD)


def attend_back(me, heads, kv, grads, logs, cosine, signed):
    return pl.pallas_call(
        attend_back_kernel,
        in_specs=[pl.BlockSpec(memory_space=pltpu.SMEM)] + whole(6),
        out_specs=whole(2),
        out_shape=[
            jax.ShapeDtypeStruct((ROWS, WIDTH_Q), BF),
            jax.ShapeDtypeStruct((8, ROWS, 512), BF),
        ],
        compiler_params=pltpu.CompilerParams(vmem_limit_bytes=56 << 20),
        cost_estimate=cost(9),
    )(me, heads, kv, grads, logs, cosine, signed)


def halves(core_ref, mine, other):
    first = core_ref[0] == 0
    return jnp.where(first, mine, other), jnp.where(first, other, mine)


def middle_kernel(
    core_ref, att_ref, x_ref, gain_ref, mine_ref, other_ref, mid_ref, scale_ref, h_ref
):
    att = att_ref[...]
    mine = jnp.dot(att, mine_ref[...], preferred_element_type=F32)
    other = jnp.dot(att, other_ref[...], preferred_element_type=F32)
    low, high = halves(core_ref, mine, other)
    low = x_ref[:, : D // 2].astype(F32) + low
    high = x_ref[:, D // 2 :].astype(F32) + high
    square = jnp.sum(low * low, axis=-1, keepdims=True) + jnp.sum(
        high * high, axis=-1, keepdims=True
    )
    scale = lax.rsqrt(square / D + NORM_EPSILON)
    scale_ref[...] = scale
    mid_ref[:, : D // 2] = low
    mid_ref[:, D // 2 :] = high
    h_ref[:ROWS, : D // 2] = (low * scale * gain_ref[:, : D // 2]).astype(BF)
    h_ref[:ROWS, D // 2 :] = (high * scale * gain_ref[:, D // 2 :]).astype(BF)
    h_ref[ROWS:] = att


def middle_of(core, attended, rows, gain, mine, other):
    return pl.pallas_call(
        middle_kernel,
        in_specs=[pl.BlockSpec(memory_space=pltpu.SMEM)]
        + whole(5),
        out_specs=whole(3),
        out_shape=[
            jax.ShapeDtypeStruct((ROWS, D), F32),
            jax.ShapeDtypeStruct((ROWS, 1), F32),
            jax.ShapeDtypeStruct((2 * ROWS, D), BF),
        ],
        compiler_params=pltpu.CompilerParams(vmem_limit_bytes=24 << 20),
        cost_estimate=cost(3),
    )(core, attended, rows, gain, mine, other)


def turning_kernel(core_ref, mid_ref, scale_ref, gain_ref, cot_ref, mine_ref, other_ref, *refs):
    mid_grad_ref, branch_ref, att_ref, gain_grad_ref, arrived, sems = refs[5:]
    copies = fetch([(refs[k], arrived.at[k]) for k in range(5)], sems)
    for copy in copies:
        copy.wait()
    grad = arrived[0].astype(F32)
    for k in range(1, 5):
        grad = grad + arrived[k].astype(F32)
    mid, scale = mid_ref[...], scale_ref[...]
    gain_grad_ref[...] = jnp.sum(grad * mid * scale, axis=0, keepdims=True)
    weighted = grad * gain_ref[...]
    mean = jnp.mean(weighted * mid, axis=-1, keepdims=True)
    grad = cot_ref[...].astype(F32) + scale * (weighted - mid * (scale * scale * mean))
    mid_grad_ref[...] = grad
    branch = grad.astype(BF)
    branch_ref[...] = branch
    mine, other = halves(core_ref, branch[:, : D // 2], branch[:, D // 2 :])
    att = contract_cols(mine, mine_ref[...]) + contract_cols(other, other_ref[...])
    att_ref[...] = att.astype(BF)


def turning(core, middle, scale, gain, cotangent, mine, other, parts):
    return pl.pallas_call(
        turning_kernel,
        in_specs=[pl.BlockSpec(memory_space=pltpu.SMEM)]
        + whole(6)
        + anywhere(5),
        out_specs=whole(4),
        out_shape=[
            jax.ShapeDtypeStruct((ROWS, D), F32),
            jax.ShapeDtypeStruct((ROWS, D), BF),
            jax.ShapeDtypeStruct((ROWS, D), BF),
            jax.ShapeDtypeStruct((1, D), F32),
        ],
        scratch_shapes=[pltpu.VMEM((5, ROWS, D), BF), pltpu.SemaphoreType.DMA((5,))],
        compiler_params=pltpu.CompilerParams(vmem_limit_bytes=32 << 20),
        cost_estimate=cost(4.2),
    )(core, middle, scale, gain, cotangent, mine, other, *parts)


def feed_kernel(held, order_ref, *refs):
    h_refs, c_ref, weights = refs[:4], refs[4], refs[5:7]
    up_w, packed, down_w, h_all, c_all, total_ref, rows_ref, sems, row_sems, in_sems = refs[-10:]
    outs = refs[7 + held : -10]
    act_refs, grad_refs, out_ref, part_refs = outs[:2], outs[2:4], outs[4], outs[5:]
    first = 4 if held else 0
    copies = []
    for side in range(2):
        for n, (rows, target) in enumerate(
            ((slice(0, SHARD), up_w), (slice(SHARD, SHARD + 96), packed))
        ):
            copy = pltpu.make_async_copy(
                weights[side].at[:, rows], target.at[side], sems.at[side, n]
            )
            copy.start()
            copies.append(copy)
    tokens = fetch(
        [(h_refs[i].at[:ROWS], rows_of(h_all, i)) for i in range(4)]
        + [(c_ref.at[order_ref[first + i]], rows_of(c_all, i)) for i in range(4)],
        in_sems,
    )
    for copy in tokens:
        copy.wait()
    for side in range(2):
        grad_ref = grad_refs[side]
        copies[2 * side].wait()
        up_now = up_w[side].reshape(D, 2 * COLS)
        gate_up = jnp.dot(h_all[...], up_now, preferred_element_type=F32)
        copies[2 * side + 1].wait()
        for g in range(8):
            for (r, c), (rows, cols) in piece_parts():
                down_w[PIECE * g + rows.start : PIECE * g + rows.stop, cols] = packed[side, g, r, c]
        grad_act = contract_cols(c_all[...], down_w[...])
        gate, up = gate_up[:, :COLS], gate_up[:, COLS:]
        sig = jax.nn.sigmoid(gate)
        silu = gate * sig
        act_refs[side][...] = (silu * up).astype(BF)
        rows = jnp.dot(act_refs[side][...], down_w[...], preferred_element_type=F32)
        grad_ref[:, :COLS] = (grad_act * up * sig * (1.0 + gate * (1.0 - sig))).astype(BF)
        grad_ref[:, COLS:] = (grad_act * silu).astype(BF)
        if side == 0:
            total_ref[...] = rows
            part = contract_cols(grad_ref[...], up_now)
        else:
            rows_ref[...] = (total_ref[...] + rows).astype(BF)
            copies = []
            for i in range(4):
                copy = pltpu.make_async_copy(
                    rows_ref.at[ROWS * i : ROWS * (i + 1)],
                    out_ref.at[order_ref[first + i]],
                    row_sems.at[i],
                )
                copy.start()
                copies.append(copy)
            part = part + contract_cols(grad_ref[...], up_now)
            for i in range(4):
                part_refs[i][...] = part[ROWS * i : ROWS * (i + 1)].astype(BF)
            for copy in copies:
                copy.wait()


def feed(order, h_blocks, cot_all, mine, other, held):
    tokens = 4 * ROWS
    at = 1 if held else 0
    widths = (COLS, COLS, 2 * COLS, 2 * COLS)
    outs = pl.pallas_call(
        functools.partial(feed_kernel, len(held)),
        grid=(1,),
        in_specs=scalars(1) + anywhere(7 + len(held)),
        out_specs=[pl.BlockSpec((tokens, w), lambda i: (at, 0)) for w in widths]
        + anywhere(1)
        + whole(4),
        out_shape=[jax.ShapeDtypeStruct((2 * tokens, w), BF) for w in widths]
        + [jax.ShapeDtypeStruct((8, ROWS, D), BF)]
        + [jax.ShapeDtypeStruct((ROWS, D), BF)] * 4,
        scratch_shapes=[
            pltpu.VMEM((2, 8, SHARD, 2 * COLS), BF),
            pltpu.VMEM((2, 8, 96, 2 * COLS), BF),
            pltpu.VMEM((COLS, D), BF),
            pltpu.VMEM((tokens, D), BF),
            pltpu.VMEM((tokens, D), BF),
            pltpu.VMEM((tokens, D), F32),
            pltpu.VMEM((tokens, D), BF),
            pltpu.SemaphoreType.DMA((2, 2)),
            pltpu.SemaphoreType.DMA((4,)),
            pltpu.SemaphoreType.DMA((8,)),
        ],
        input_output_aliases={8 + k: k for k in range(len(held))},
        compiler_params=pltpu.CompilerParams(vmem_limit_bytes=56 << 20),
        cost_estimate=cost(21),
    )(order, *h_blocks, cot_all, mine, other, *held)
    return tuple(outs[:5]), outs[5:]


def assemble_kernel(dq_ref, dkv_ref, branch_ref, cos_ref, sin_ref, both_ref, out_ref):
    dkv = dkv_ref[0].astype(F32)
    for k in range(1, 8):
        dkv = dkv + dkv_ref[k].astype(F32)
    for h in range(2):
        u = dkv[:, HEAD * h : HEAD * (h + 1)]
        u = u * cos_ref[...] - pltpu.roll(u, HEAD // 2, 1) * sin_ref[...]
        u = u.astype(BF)
        both_ref[6, :, HEAD * h : HEAD * (h + 1)] = u
        out_ref[:, WIDTH_Q + HEAD * h : WIDTH_Q + HEAD * (h + 1)] = u
    u = dkv[:, 256:].astype(BF)
    both_ref[7, :, :256] = u
    out_ref[:, WIDTH_Q + 256 :] = u
    for q in range(6):
        u = dq_ref[:, 256 * q : 256 * (q + 1)]
        both_ref[q, :, :256] = u
        out_ref[:, 256 * q : 256 * (q + 1)] = u
        both_ref[q, :, 256:] = branch_ref[:, 256 * q : 256 * (q + 1)]
    for q in range(6, 8):
        both_ref[q, :, 256:] = jnp.zeros((ROWS, 256), BF)


def assemble(dq, dkv, branch, cosine, signed):
    return pl.pallas_call(
        assemble_kernel,
        in_specs=whole(5),
        out_specs=whole(2),
        out_shape=[
            jax.ShapeDtypeStruct((8, ROWS, 512), BF),
            jax.ShapeDtypeStruct((ROWS, QKV), BF),
        ],
        compiler_params=pltpu.CompilerParams(vmem_limit_bytes=16 << 20),
        cost_estimate=cost(1.2),
    )(dq, dkv, branch, cosine, signed)


def on_device(hidden_in, norm_attn, w_qkv, b_qkv, w_out, norm_mlp, w_gate_up, w_down, cotangent):
    core = lax.axis_index("c")
    plane = lax.axis_index(PLANE)
    replica = lax.axis_index(REPLICA)
    group = lax.axis_index(GROUP)
    yl, zz = lax.axis_index("yl"), lax.axis_index("z")
    yh, xx = lax.axis_index("yh"), lax.axis_index("x")
    first_row = group * ROWS
    works = replica < ROLES
    role = jnp.minimum(replica, ROLES - 1)

    x_blocks = send_out(hidden_in[0], PLANE, True)
    pad = jnp.zeros((64,), BF)
    small = jnp.concatenate([b_qkv, norm_attn, pad, norm_mlp, pad]).reshape(3, 256)
    columns = lax.dynamic_slice(w_qkv, (0, plane * 256), (SHARD, 256))
    columns = jnp.concatenate([columns, small, jnp.zeros((13, 256), BF)], axis=0)
    columns = gather_direct(after(columns, *x_blocks[1:5]), GROUP)
    columns = after(columns, *x_blocks[5:])
    qkv_role = columns[:, :SHARD].reshape(D, 256)
    bias_full = columns[:, SHARD : SHARD + 1].astype(F32)
    gain_one = columns[:, SHARD + 1, :SHARD].reshape(1, D).astype(F32)
    gain_two = columns[:, SHARD + 2, :SHARD].reshape(1, D).astype(F32)

    out_half = lax.dynamic_slice(w_out, (0, core * 768), (SHARD, 768))
    out_mine = lax.all_gather(out_half, GROUP, axis=0, tiled=True)
    piece = lax.dynamic_slice(w_down, (role * PIECE, 0), (PIECE, D))
    piece = lax.ppermute(piece, EVERY, down_pairs())
    (packed,) = call(
        pack_kernel,
        1,
        [((SHARD + 96, 2 * COLS), BF)],
        scalars(1) + whole(3),
        works.astype(jnp.int32).reshape(1),
        lax.dynamic_slice(w_gate_up, (0, role * COLS), (SHARD, COLS)),
        lax.dynamic_slice(w_gate_up, (0, FF + role * COLS), (SHARD, COLS)),
        piece,
    )
    feed_mine = lax.all_gather(after(packed, x_blocks[1]), GROUP, axis=0)

    cosine, signed = rope_tables(first_row, ROWS, HEAD)
    turns = plane < 7
    order = jnp.stack([place(yl, zz, o, -1) for o in ALL_OFFSETS]).astype(jnp.int32)
    normed_one_all, heads = project(
        order,
        gain_one,
        qkv_role,
        pick(bias_full, plane),
        jnp.where(turns, cosine, 1.0),
        jnp.where(turns, signed, 0.0),
        x_blocks,
    )

    grad_out = cotangent[0]
    cot_blocks = send_out(after(grad_out, *x_blocks), PLANE, True)
    heads = after(heads, *cot_blocks[1:5])
    heads = lax.all_to_all(heads, PLANE, 0, 0, tiled=True)
    out_other = swap(after(out_mine, heads))
    kv_own = jnp.concatenate([heads[6], heads[7]], axis=1)
    kv_all = gather_direct(kv_own, GROUP)
    kv_all = after(kv_all, *cot_blocks)
    cot_all = arrange(order, cot_blocks)
    me = group.astype(jnp.int32).reshape(1)
    attended, logs = attend(me, heads, kv_all)
    which = core.astype(jnp.int32).reshape(1)
    middle, scale_two, normed_two = middle_of(
        which, attended, hidden_in[0], gain_two, out_mine, out_other
    )

    h_blocks = send_out(normed_two, PLANE)
    feed_other = swap(after(feed_mine, *h_blocks[1:3]))
    qkv_half = lax.dynamic_slice(w_qkv, (0, core * 1024), (SHARD, 1024))
    qkv_mine = lax.all_gather(after(qkv_half, normed_two), GROUP, axis=0, tiled=True)
    held, back_blocks = (), {}
    for part in (slice(0, 4), slice(4, 8)):
        held, parts = feed(order, h_blocks[part], cot_all, feed_mine, feed_other, held)
        for o, block in zip(ALL_OFFSETS[part], parts):
            back_blocks[back(o)] = block
    second_parts, _, round_sums = send_parts(back_blocks, PLANE)

    held_h = after(tuple(h_blocks), parts, qkv_mine)
    given = weight_grads(order, held_h, cot_all, held[3], held[1])
    group_order = jnp.stack([place(yh, xx, o) for o in ALL_OFFSETS]).astype(jnp.int32)
    merged = merged_grads(
        order, group_order, held_h, cot_all, held[2], held[0], swap(given)
    )
    second_parts = after(second_parts, merged)
    grad_middle, grad_branch, grad_attended, gain_two_grad = turning(
        which, middle, scale_two, gain_two, grad_out, out_mine, out_other, second_parts
    )
    grad_q, grad_kv = attend_back(me, heads, kv_all, grad_attended, logs, cosine, signed)
    mlp_parts, mlp_first, _ = send_parts(
        dict(zip(ALL_OFFSETS, merged)), GROUP
    )
    grad_kv = after(grad_kv, *mlp_first)
    grad_kv = lax.all_to_all(grad_kv, GROUP, 0, 0, tiled=True)

    out_rows = after(held[4], *second_parts).reshape(8 * ROWS, D)
    out_rows = lax.psum_scatter(out_rows, PLANE, scatter_dimension=0, tiled=True)
    result = (middle + out_rows.astype(F32)).astype(BF)[None]

    both, grad_projected = assemble(grad_q, grad_kv, grad_branch, cosine, signed)
    qkv_other = swap(after(qkv_mine, both))
    assembled = both
    both = lax.all_to_all(both, PLANE, 0, 0, tiled=True)

    grad_in, gain_one_grad = finish(
        which, grad_projected, qkv_mine, qkv_other, hidden_in[0], gain_one, grad_middle
    )
    keep, give, bias_grad = attention_grads(which, order, normed_one_all, after(both, gain_one_grad, *mlp_parts), h_blocks)
    gains = jnp.stack([gain_one_grad[0], gain_two_grad[0]]).astype(BF).reshape(2, 8, SHARD)
    gains = jnp.pad(gains.transpose(1, 0, 2), ((0, 0), (0, 14), (0, 64)))
    (payload,) = call(
        payload_kernel, 1.4,
        [((8, SHARD + 16, 256), BF)],
        whole(4),
        keep,
        swap(give),
        gains,
        bias_grad,
    )
    mlp_grad = total(after(tuple(mlp_parts), out_rows)).astype(BF)
    down_grad = lax.ppermute(mlp_grad[SHARD:], EVERY, [(t, s) for s, t in down_pairs()])
    mlp_grad = jnp.concatenate([mlp_grad[:SHARD], down_grad], axis=0)
    payload = lax.all_to_all(payload, GROUP, 0, 0, tiled=True)
    grad_blocks = send_out(mlp_grad, PLANE, hold=(payload,))
    other_blocks = [swap(b) for b in grad_blocks]
    feed_grads = write_grads(which, order, grad_blocks, other_blocks, 0, 5, ())
    gate_up_grad, down_grad = write_grads(which, order, grad_blocks, other_blocks, 5, 8, feed_grads)


    (payload,) = call(sum_kernel, 1, [((8, SHARD + 16, 256), BF)], whole(1), payload)
    mine = lax.all_to_all(payload, PLANE, 0, 0, tiled=True)
    mine = after(mine, *feed_grads)
    other = swap(mine)
    qkv_grad, out_grad, gains, bias_grad = call(
        last_kernel,
        3,
        [((SHARD, QKV), F32), ((SHARD, D), F32), ((16, 256), F32), ((16, 256), F32)],
        [pl.BlockSpec(memory_space=pltpu.SMEM)] * 2 + whole(2),
        which,
        me,
        mine,
        other,
    )

    return (
        result,
        grad_in[None],
        gains[0, :SHARD],
        qkv_grad,
        bias_grad[2],
        out_grad,
        gains[1, :SHARD],
        gate_up_grad,
        down_grad,
    )


def solution(mesh):
    fine = Mesh(mesh.devices.reshape(2, 4, 2, 4, 2), EVERY)
    tokens = P(REPLICA, GROUP, None)
    matrix = P(GROUP, None)
    vector = P(GROUP)
    return jax.shard_map(
        on_device,
        mesh=fine,
        in_specs=(tokens, vector, matrix, vector, matrix, vector, matrix, matrix, tokens),
        out_specs=(tokens, tokens, vector, matrix, vector, matrix, vector, matrix, matrix),
        check_vma=False,
    )
```

```python
import functools

import jax
import jax.numpy as jnp
from jax import lax
from jax.experimental import pallas as pl
from jax.experimental.pallas import tpu as pltpu
from jax.sharding import Mesh, PartitionSpec as P

D = 1536
HEADS = 12
KV_HEADS = 2
HEAD = 128
FF = 8960
QKV = 2048
ROWS = 128
GROUPS = HEADS // KV_HEADS
WIDTH_Q = HEADS * HEAD
WIDTH_K = KV_HEADS * HEAD
ROLES = 14
COLS = FF // ROLES
SHARD = D // 8
PIECE = COLS // 8
PIECES = FF // 8 // PIECE

NORM_EPSILON = 1e-06
ROPE_BASE = 1000000.0
BF = jnp.bfloat16


def cost(micros):
    return pl.CostEstimate(flops=int(micros * SCALE), bytes_accessed=1000, transcendentals=0)


SCALE = 0.58e9
F32 = jnp.float32

GROUP = ("yh", "x")
PLANE = ("yl", "z")
REPLICA = ("yl", "z", "c")
GROUP_CORE = ("yh", "x", "c")
EVERY = ("yh", "x", "yl", "z", "c")

ALL_OFFSETS = ((0, 0), (0, 1), (0, 3), (1, 0), (0, 2), (1, 1), (1, 3), (1, 2))


def shift_pairs(offset):
    dy, dx = offset
    return [
        (y * 4 + x, ((y + dy) % 2) * 4 + (x + dx) % 4) for y in range(2) for x in range(4)
    ]


def back(offset):
    return (offset[0], (4 - offset[1]) % 4)


def send(block, axes, offset):
    return lax.ppermute(block, axes, shift_pairs(offset))


def send_out(block, axes, row=False, hold=()):
    one, three = send(block, axes, (0, 1)), send(block, axes, (0, 3))
    across, two = send(block, axes, (1, 0)), send(block, axes, (0, 2))
    across, two = after((across, two), *hold)
    return [
        block,
        one,
        three,
        across,
        two,
        send(across, axes, (0, 1)),
        send(across, axes, (0, 3)),
        send(across, axes, (0, 2)) if row else send(two, axes, (1, 0)),
    ]


def send_parts(blocks, axes, hold=()):
    first = (
        send(blocks[1, 1], axes, (0, 1)),
        send(blocks[1, 3], axes, (0, 3)),
        send(blocks[1, 2], axes, (1, 0)),
    )
    from_one, from_three, from_across = after(first, *hold)
    two = (blocks[0, 2].astype(F32) + from_across.astype(F32)).astype(BF)
    across = total([blocks[1, 0], from_one, from_three]).astype(BF)
    parts = [
        blocks[0, 0],
        send(blocks[0, 1], axes, (0, 1)),
        send(blocks[0, 3], axes, (0, 3)),
        send(two, axes, (0, 2)),
        send(across, axes, (1, 0)),
    ]
    return parts, first, (two, across)


def after(value, *done):
    return lax.optimization_barrier((value,) + done)[0] if done else value


def total(blocks):
    out = blocks[0].astype(F32)
    for b in blocks[1:]:
        out = out + b.astype(F32)
    return out


def down_pairs():
    pairs = []
    for r in range(ROLES):
        for g in range(8):
            piece = 8 * r + g
            pairs.append(((piece // PIECES) * 16 + piece % PIECES, g * 16 + r))
    return pairs


def rope_tables(first_row, row_count, head_size):
    half_width = head_size // 2
    position = (first_row + jnp.arange(row_count, dtype=jnp.int32)).astype(F32)
    frequency = jnp.power(
        ROPE_BASE, -(jnp.arange(half_width, dtype=jnp.int32).astype(F32) * 2.0) / head_size
    )
    angles = position[:, None] * frequency[None, :]
    cosine = jnp.concatenate([jnp.cos(angles), jnp.cos(angles)], axis=-1)
    signed = jnp.concatenate([-jnp.sin(angles), jnp.sin(angles)], axis=-1)
    return (cosine, signed)


def contract_rows(left_side, right_side):
    return lax.dot_general(
        left_side, right_side, (((0,), (0,)), ((), ())), preferred_element_type=F32
    )


def contract_cols(left_side, right_side):
    return lax.dot_general(
        left_side, right_side, (((1,), (1,)), ((), ())), preferred_element_type=F32
    )


def swap(block):
    return lax.ppermute(block, "c", [(0, 1), (1, 0)])


def gather_direct(block, axes):
    return lax.all_to_all(jnp.broadcast_to(block[None], (8,) + block.shape), axes, 0, 0, tiled=True)


def place(y, x, offset, sign=1):
    return ((y + sign * offset[0]) % 2) * 4 + (x + sign * offset[1]) % 4


def pick(blocks, index):
    return lax.dynamic_index_in_dim(blocks, index, 0, keepdims=False)


def piece_parts():
    for i in range(5):
        for j in range(6):
            low, high = max(96 * i, 80 * j), min(96 * (i + 1), 80 * (j + 1))
            if low < high:
                yield (
                    (slice(low - 96 * i, high - 96 * i), slice(256 * i, 256 * (i + 1))),
                    (slice(low - 80 * j, high - 80 * j), slice(256 * j, 256 * (j + 1))),
                )


def call(kernel, micros, out_shape, in_specs, *args, vmem=48, **more):
    return pl.pallas_call(
        kernel,
        in_specs=in_specs,
        out_specs=[pl.BlockSpec(memory_space=pltpu.VMEM)] * len(out_shape),
        out_shape=[jax.ShapeDtypeStruct(shape, kind) for shape, kind in out_shape],
        compiler_params=pltpu.CompilerParams(vmem_limit_bytes=vmem << 20),
        cost_estimate=cost(micros),
        **more,
    )(*args)


def pack_kernel(works_ref, gate_ref, up_ref, piece_ref, out_ref):
    works = works_ref[0] > 0
    gate, up = gate_ref[...], up_ref[...]
    out_ref[:SHARD, :COLS] = jnp.where(works, gate, jnp.zeros_like(gate))
    out_ref[:SHARD, COLS:] = jnp.where(works, up, jnp.zeros_like(up))
    for (r, c), (rows, cols) in piece_parts():
        out_ref[SHARD + r.start : SHARD + r.stop, c] = piece_ref[rows, cols]


def arrange_kernel(order_ref, *refs):
    for k in range(8):
        refs[8][order_ref[k]] = refs[k][...]


def arrange(order, blocks):
    return call(
        arrange_kernel,
        2,
        [((8,) + blocks[0].shape, BF)],
        [pl.BlockSpec(memory_space=pltpu.SMEM)] + whole(8),
        order,
        *blocks,
    )[0]


def packed_grads(order_ref, refs, up_sum, down_sum, scratch):
    h_all, c_all, grad, act, sems = scratch
    c_ref, grad_ref, act_ref = refs[8:11]
    copies = fetch(
        [(grad_ref, grad)]
        + [(refs[k].at[:ROWS], rows_of(h_all, k)) for k in range(8)]
        + [(act_ref, act)]
        + [(c_ref.at[order_ref[k]], rows_of(c_all, k)) for k in range(8)],
        sems,
    )
    for copy in copies[:9]:
        copy.wait()
    up_sum[...] = contract_rows(h_all[...], grad[...]).reshape(8, SHARD, 2 * COLS).astype(BF)
    for copy in copies[9:]:
        copy.wait()
    down_sum[...] = contract_rows(act[...], c_all[...]).astype(BF)


GRAD_SCRATCH = [
    pltpu.VMEM((8 * ROWS, D), BF),
    pltpu.VMEM((8 * ROWS, D), BF),
    pltpu.VMEM((8 * ROWS, 2 * COLS), BF),
    pltpu.VMEM((8 * ROWS, COLS), BF),
    pltpu.SemaphoreType.DMA((18,)),
]


def weight_kernel(order_ref, *refs):
    out_ref, down_sum = refs[11:13]
    packed_grads(order_ref, refs, out_ref.at[:, :SHARD], down_sum, refs[13:])
    for g in range(8):
        for (r, c), (rows, cols) in piece_parts():
            out_ref[g, SHARD + r.start : SHARD + r.stop, c] = down_sum[
                PIECE * g + rows.start : PIECE * g + rows.stop, cols
            ]


def weight_grads(order, h_blocks, cot_all, grads, acts):
    return call(
        weight_kernel,
        10.7,
        [((8, SHARD + 96, 2 * COLS), BF)],
        scalars(1) + anywhere(11),
        order,
        *h_blocks,
        cot_all,
        grads,
        acts,
        scratch_shapes=[pltpu.VMEM((COLS, D), BF)] + GRAD_SCRATCH,
    )[0]


def merge_kernel(token_order_ref, order_ref, *refs):
    given_ref, outs, (up_sum, down_sum, given, sem) = refs[11], refs[12:20], refs[20:24]
    copy = fetch([(given_ref, given)], sem)[0]
    packed_grads(token_order_ref, refs, up_sum, down_sum, refs[24:])
    copy.wait()
    for k in range(8):
        g = order_ref[k]
        outs[k][:SHARD] = (up_sum[g].astype(F32) + given[g, :SHARD].astype(F32)).astype(BF)
        first = pl.multiple_of(g * PIECE, PIECE)
        for (r, c), (rows, cols) in piece_parts():
            to = slice(SHARD + r.start, SHARD + r.stop)
            own = down_sum[pl.ds(first + rows.start, rows.stop - rows.start), cols]
            outs[k][to, c] = (own.astype(F32) + given[g, to, c].astype(F32)).astype(BF)


def merged_grads(token_order, order, h_blocks, cot_all, grads, acts, given):
    return call(
        merge_kernel,
        15,
        [((SHARD + 96, 2 * COLS), BF)] * 8,
        scalars(2) + anywhere(12),
        token_order,
        order,
        *h_blocks,
        cot_all,
        grads,
        acts,
        given,
        vmem=56,
        scratch_shapes=[
            pltpu.VMEM((8, SHARD, 2 * COLS), BF),
            pltpu.VMEM((COLS, D), BF),
            pltpu.VMEM((8, SHARD + 96, 2 * COLS), BF),
            pltpu.SemaphoreType.DMA((1,)),
        ]
        + GRAD_SCRATCH,
    )


def finish_kernel(
    core_ref, grad_ref, mine_ref, other_ref, x_ref, gain_ref, mid_ref, out_ref, gain_grad_ref
):
    half = QKV // 2
    grad = grad_ref[...]
    mine, other = halves(core_ref, grad[:, :half], grad[:, half:])
    normed = contract_cols(mine, mine_ref[...]) + contract_cols(other, other_ref[...])
    x = x_ref[...].astype(F32)
    scale = lax.rsqrt(jnp.mean(x * x, axis=-1, keepdims=True) + NORM_EPSILON)
    gain_grad_ref[...] = jnp.sum(normed * x * scale, axis=0, keepdims=True)
    weighted = normed * gain_ref[...]
    mean = jnp.mean(weighted * x, axis=-1, keepdims=True)
    out_ref[...] = mid_ref[...] + scale * (weighted - x * (scale * scale * mean))


def finish(core, grad_projected, mine, other, rows, gain, grad_middle):
    return call(
        finish_kernel, 5,
        [((ROWS, D), F32), ((1, D), F32)],
        [pl.BlockSpec(memory_space=pltpu.SMEM)] + whole(6),
        core,
        grad_projected,
        mine,
        other,
        rows,
        gain,
        grad_middle,
    )


def attention_grads_kernel(core_ref, order_ref, normed_ref, both_ref, *refs):
    keep_ref, give_ref, bias_ref, att_all, sems = refs[8:]
    copies = fetch(
        [(refs[k].at[ROWS:], att_all.at[order_ref[k]]) for k in range(8)], sems
    )
    both = both_ref[...].reshape(8 * ROWS, 512)
    role = both[:, :256]
    bias_ref[...] = jnp.sum(role.astype(F32), axis=0, keepdims=True)
    qkv = contract_rows(normed_ref[...].reshape(8 * ROWS, D), role)
    for copy in copies:
        copy.wait()
    out = contract_rows(att_all[...].reshape(8 * ROWS, D), both[:, 256:])
    keep, give = halves(core_ref, qkv, out)
    keep_ref[...] = keep
    give_ref[...] = give.astype(BF)


def attention_grads(core, order, normed, both, bundles):
    return call(
        attention_grads_kernel,
        5,
        [((D, 256), F32), ((D, 256), BF), ((1, 256), F32)],
        scalars(2) + whole(2) + anywhere(8),
        core,
        order,
        normed,
        both,
        *bundles,
        scratch_shapes=[pltpu.VMEM((8, ROWS, D), BF), pltpu.SemaphoreType.DMA((8,))],
    )


def last_kernel(core_ref, group_ref, mine_ref, other_ref, qkv_ref, out_ref, gain_ref, bias_ref):
    gains = jnp.zeros((16, 256), F32)
    for q in range(8):
        mine, other = mine_ref[q].astype(F32), other_ref[q].astype(F32)
        qkv, out = halves(core_ref, mine[:SHARD], other[:SHARD])
        qkv_ref[:, 256 * q : 256 * (q + 1)] = qkv
        if q < 6:
            out_ref[:, 256 * q : 256 * (q + 1)] = out
        gains = gains + mine[SHARD:] + other[SHARD:]
    gain_ref[...] = gains
    g = group_ref[0]
    bias_ref[...] = mine_ref[g, SHARD:].astype(F32) + other_ref[g, SHARD:].astype(F32)


def payload_kernel(keep_ref, other_ref, extra_ref, bias_ref, out_ref):
    row = lax.broadcasted_iota(jnp.int32, (16, 256), 0)
    bias = bias_ref[...].astype(BF).astype(F32)
    for g in range(8):
        rows = slice(SHARD * g, SHARD * (g + 1))
        out_ref[g, :SHARD] = (keep_ref[rows] + other_ref[rows].astype(F32)).astype(BF)
        extra = extra_ref[g].astype(F32)
        out_ref[g, SHARD:] = jnp.where(row == 2, bias, extra).astype(BF)


def sum_kernel(in_ref, out_ref):
    rows = in_ref[0].astype(F32)
    for g in range(1, 8):
        rows = rows + in_ref[g].astype(F32)
    rows = rows.astype(BF)
    for g in range(8):
        out_ref[g] = rows


def write_kernel(low, count, held, core_ref, order_ref, *refs):
    blocks = refs[: 2 * count]
    wide_out, down_out, narrow, wide, down, in_sems, sems = refs[2 * count + held :]
    arrivals = fetch([(blocks[n], narrow.at[n]) for n in range(2 * count)], in_sems)
    for start in (True, False):
        for n in range(2 * count):
            chip = order_ref[low + n % count]
            role = 2 * chip + (core_ref[0] if n < count else 1 - core_ref[0])
            if start:
                arrivals[n].wait()

            @pl.when(chip < ROLES // 2)
            def _(n=n, role=role):
                copies = [
                    pltpu.make_async_copy(
                        wide.at[n, :, :COLS],
                        wide_out.at[:, pl.ds(pl.multiple_of(role * COLS, 128), COLS)],
                        sems.at[n, 0],
                    ),
                    pltpu.make_async_copy(
                        wide.at[n, :, COLS:],
                        wide_out.at[:, pl.ds(pl.multiple_of(FF + role * COLS, 128), COLS)],
                        sems.at[n, 1],
                    ),
                    pltpu.make_async_copy(
                        down.at[n],
                        down_out.at[pl.ds(pl.multiple_of(role * PIECE, PIECE), PIECE)],
                        sems.at[n, 2],
                    ),
                ]
                if start:
                    wide[n] = narrow[n, :SHARD].astype(F32)
                    copies[0].start()
                    copies[1].start()
                    for (r, c), (rows, cols) in piece_parts():
                        down[n, rows, cols] = narrow[
                            n, SHARD + r.start : SHARD + r.stop, c
                        ].astype(F32)
                    copies[2].start()
                else:
                    for copy in copies:
                        copy.wait()


def write_grads(core, order, mine, other, low, high, held):
    count = high - low
    return pl.pallas_call(
        functools.partial(write_kernel, low, count, len(held)),
        in_specs=scalars(2) + anywhere(2 * count + len(held)),
        out_specs=anywhere(2),
        out_shape=[
            jax.ShapeDtypeStruct((SHARD, 2 * FF), F32),
            jax.ShapeDtypeStruct((FF // 8, D), F32),
        ],
        scratch_shapes=[
            pltpu.VMEM((2 * count, SHARD + 96, 2 * COLS), BF),
            pltpu.VMEM((2 * count, SHARD, 2 * COLS), F32),
            pltpu.VMEM((2 * count, PIECE, D), F32),
            pltpu.SemaphoreType.DMA((2 * count,)),
            pltpu.SemaphoreType.DMA((2 * count, 3)),
        ],
        input_output_aliases={2 + 2 * count + k: k for k in range(len(held))},
        compiler_params=pltpu.CompilerParams(vmem_limit_bytes=48 << 20),
        cost_estimate=cost(2 * count),
    )(core, order, *mine[low:high], *other[low:high], *held)


def project_kernel(order_ref, gain_ref, w_ref, bias_ref, cos_ref, sin_ref, *refs):
    normed_ref, heads_ref, x_all, sems = refs[8:]
    copies = fetch([(refs[k], x_all.at[k]) for k in range(8)], sems)
    for k in range(8):
        copies[k].wait()
        rows = x_all[k].astype(F32)
        scale = lax.rsqrt(jnp.mean(rows * rows, axis=-1, keepdims=True) + NORM_EPSILON)
        normed = (rows * scale * gain_ref[...]).astype(BF)
        at = order_ref[k]
        normed_ref[at] = normed
        out = jnp.dot(normed, w_ref[...], preferred_element_type=F32) + bias_ref[...]
        for h in range(2):
            u = out[:, HEAD * h : HEAD * (h + 1)]
            u = u * cos_ref[...] + pltpu.roll(u, HEAD // 2, 1) * sin_ref[...]
            heads_ref[at, :, HEAD * h : HEAD * (h + 1)] = u.astype(BF)


def whole(count):
    return [pl.BlockSpec(memory_space=pltpu.VMEM)] * count


def scalars(count):
    return [pl.BlockSpec(memory_space=pltpu.SMEM)] * count


def anywhere(count):
    return [pl.BlockSpec(memory_space=pl.ANY)] * count


def fetch(pairs, sems):
    copies = [
        pltpu.make_async_copy(source, target, sems.at[k]) for k, (source, target) in enumerate(pairs)
    ]
    for copy in copies:
        copy.start()
    return copies


def rows_of(ref, k):
    return ref.at[ROWS * k : ROWS * (k + 1)]


def project(order, gain, weight, bias, cosine, signed, blocks):
    return pl.pallas_call(
        project_kernel,
        in_specs=scalars(1) + whole(5) + anywhere(8),
        out_specs=whole(2),
        out_shape=[
            jax.ShapeDtypeStruct((8, ROWS, D), BF),
            jax.ShapeDtypeStruct((8, ROWS, 256), BF),
        ],
        scratch_shapes=[pltpu.VMEM((8, ROWS, D), BF), pltpu.SemaphoreType.DMA((8,))],
        compiler_params=pltpu.CompilerParams(vmem_limit_bytes=32 << 20),
        cost_estimate=cost(4),
    )(order, gain, weight, bias, cosine, signed, *blocks)


def head_stack(ref, side):
    return jnp.concatenate(
        [
            ref[h // 2, :, HEAD * (h % 2) : HEAD * (h % 2 + 1)]
            for h in range(GROUPS * side, GROUPS * (side + 1))
        ],
        axis=0,
    )


def scores_of(me_ref, queries, keys):
    raw = lax.dot_general(
        queries, keys, (((1,), (1,)), ((), ())), preferred_element_type=F32
    )
    raw = raw.reshape(GROUPS, ROWS, 8 * ROWS) * HEAD ** (-0.5)
    row = me_ref[0] * ROWS + lax.broadcasted_iota(jnp.int32, (ROWS, 8 * ROWS), 0)
    col = lax.broadcasted_iota(jnp.int32, (ROWS, 8 * ROWS), 1)
    return jnp.where((col <= row)[None], raw, -1e30)


def attend_kernel(me_ref, heads_ref, kv_ref, out_ref, log_ref):
    kv = kv_ref[...].reshape(8 * ROWS, 512)
    for side in range(2):
        keys = kv[:, HEAD * side : HEAD * (side + 1)]
        values = kv[:, 256 + HEAD * side : 256 + HEAD * (side + 1)]
        scores = scores_of(me_ref, head_stack(heads_ref, side), keys)
        top = jnp.max(scores, axis=-1, keepdims=True)
        exponent = jnp.exp(scores - top)
        row_total = jnp.sum(exponent, axis=-1, keepdims=True)
        mixed = jnp.dot(
            exponent.astype(BF).reshape(GROUPS * ROWS, 8 * ROWS),
            values,
            preferred_element_type=F32,
        ).reshape(GROUPS, ROWS, HEAD)
        mixed = mixed / row_total
        logs = top + jnp.log(row_total)
        for i in range(GROUPS):
            h = GROUPS * side + i
            out_ref[:, HEAD * h : HEAD * (h + 1)] = mixed[i].astype(BF)
            log_ref[h] = logs[i]


def attend(me, heads, kv):
    return pl.pallas_call(
        attend_kernel,
        in_specs=[pl.BlockSpec(memory_space=pltpu.SMEM)] + whole(2),
        out_specs=whole(2),
        out_shape=[
            jax.ShapeDtypeStruct((ROWS, WIDTH_Q), BF),
            jax.ShapeDtypeStruct((HEADS, ROWS, 1), F32),
        ],
        compiler_params=pltpu.CompilerParams(vmem_limit_bytes=48 << 20),
        cost_estimate=cost(5),
    )(me, heads, kv)


def attend_back_kernel(
    me_ref, heads_ref, kv_ref, grad_ref, log_ref, cos_ref, sin_ref, dq_ref, dkv_ref
):
    kv = kv_ref[...].reshape(8 * ROWS, 512)
    for side in range(2):
        keys = kv[:, HEAD * side : HEAD * (side + 1)]
        values = kv[:, 256 + HEAD * side : 256 + HEAD * (side + 1)]
        queries = head_stack(heads_ref, side)
        grads = jnp.concatenate(
            [
                grad_ref[:, HEAD * h : HEAD * (h + 1)]
                for h in range(GROUPS * side, GROUPS * (side + 1))
            ],
            axis=0,
        )
        scores = scores_of(me_ref, queries, keys)
        probs = jnp.exp(scores - log_ref[GROUPS * side : GROUPS * (side + 1)])
        grad_probs = contract_cols(grads, values).reshape(GROUPS, ROWS, 8 * ROWS)
        inner = jnp.sum(probs * grad_probs, axis=-1, keepdims=True)
        grad_scores = (probs * (grad_probs - inner)).astype(BF)
        grad_scores = grad_scores.reshape(GROUPS * ROWS, 8 * ROWS)
        probs_low = probs.astype(BF).reshape(GROUPS * ROWS, 8 * ROWS)
        dq = jnp.dot(grad_scores, keys, preferred_element_type=F32) * HEAD ** (-0.5)
        dk = contract_rows(grad_scores, queries) * HEAD ** (-0.5)
        dv = contract_rows(probs_low, grads)
        for i in range(GROUPS):
            h = GROUPS * side + i
            u = dq[ROWS * i : ROWS * (i + 1)]
            u = u * cos_ref[...] - pltpu.roll(u, HEAD // 2, 1) * sin_ref[...]
            dq_ref[:, HEAD * h : HEAD * (h + 1)] = u.astype(BF)
        low, high = HEAD * side, HEAD * (side + 1)
        dkv_ref[:, :, low:high] = dk.astype(BF).reshape(8, ROWS, HEAD)
        dkv_ref[:, :, 256 + low : 256 + high] = dv.astype(BF).reshape(8, ROWS, HEAD)


def attend_back(me, heads, kv, grads, logs, cosine, signed):
    return pl.pallas_call(
        attend_back_kernel,
        in_specs=[pl.BlockSpec(memory_space=pltpu.SMEM)] + whole(6),
        out_specs=whole(2),
        out_shape=[
            jax.ShapeDtypeStruct((ROWS, WIDTH_Q), BF),
            jax.ShapeDtypeStruct((8, ROWS, 512), BF),
        ],
        compiler_params=pltpu.CompilerParams(vmem_limit_bytes=56 << 20),
        cost_estimate=cost(9),
    )(me, heads, kv, grads, logs, cosine, signed)


def halves(core_ref, mine, other):
    first = core_ref[0] == 0
    return jnp.where(first, mine, other), jnp.where(first, other, mine)


def middle_kernel(
    core_ref, att_ref, x_ref, gain_ref, mine_ref, other_ref, mid_ref, scale_ref, h_ref
):
    att = att_ref[...]
    mine = jnp.dot(att, mine_ref[...], preferred_element_type=F32)
    other = jnp.dot(att, other_ref[...], preferred_element_type=F32)
    low, high = halves(core_ref, mine, other)
    low = x_ref[:, : D // 2].astype(F32) + low
    high = x_ref[:, D // 2 :].astype(F32) + high
    square = jnp.sum(low * low, axis=-1, keepdims=True) + jnp.sum(
        high * high, axis=-1, keepdims=True
    )
    scale = lax.rsqrt(square / D + NORM_EPSILON)
    scale_ref[...] = scale
    mid_ref[:, : D // 2] = low
    mid_ref[:, D // 2 :] = high
    h_ref[:ROWS, : D // 2] = (low * scale * gain_ref[:, : D // 2]).astype(BF)
    h_ref[:ROWS, D // 2 :] = (high * scale * gain_ref[:, D // 2 :]).astype(BF)
    h_ref[ROWS:] = att


def middle_of(core, attended, rows, gain, mine, other):
    return pl.pallas_call(
        middle_kernel,
        in_specs=[pl.BlockSpec(memory_space=pltpu.SMEM)]
        + whole(5),
        out_specs=whole(3),
        out_shape=[
            jax.ShapeDtypeStruct((ROWS, D), F32),
            jax.ShapeDtypeStruct((ROWS, 1), F32),
            jax.ShapeDtypeStruct((2 * ROWS, D), BF),
        ],
        compiler_params=pltpu.CompilerParams(vmem_limit_bytes=24 << 20),
        cost_estimate=cost(3),
    )(core, attended, rows, gain, mine, other)


def turning_kernel(core_ref, mid_ref, scale_ref, gain_ref, cot_ref, mine_ref, other_ref, *refs):
    mid_grad_ref, branch_ref, att_ref, gain_grad_ref, arrived, sems = refs[5:]
    copies = fetch([(refs[k], arrived.at[k]) for k in range(5)], sems)
    for copy in copies:
        copy.wait()
    grad = arrived[0].astype(F32)
    for k in range(1, 5):
        grad = grad + arrived[k].astype(F32)
    mid, scale = mid_ref[...], scale_ref[...]
    gain_grad_ref[...] = jnp.sum(grad * mid * scale, axis=0, keepdims=True)
    weighted = grad * gain_ref[...]
    mean = jnp.mean(weighted * mid, axis=-1, keepdims=True)
    grad = cot_ref[...].astype(F32) + scale * (weighted - mid * (scale * scale * mean))
    mid_grad_ref[...] = grad
    branch = grad.astype(BF)
    branch_ref[...] = branch
    mine, other = halves(core_ref, branch[:, : D // 2], branch[:, D // 2 :])
    att = contract_cols(mine, mine_ref[...]) + contract_cols(other, other_ref[...])
    att_ref[...] = att.astype(BF)


def turning(core, middle, scale, gain, cotangent, mine, other, parts):
    return pl.pallas_call(
        turning_kernel,
        in_specs=[pl.BlockSpec(memory_space=pltpu.SMEM)]
        + whole(6)
        + anywhere(5),
        out_specs=whole(4),
        out_shape=[
            jax.ShapeDtypeStruct((ROWS, D), F32),
            jax.ShapeDtypeStruct((ROWS, D), BF),
            jax.ShapeDtypeStruct((ROWS, D), BF),
            jax.ShapeDtypeStruct((1, D), F32),
        ],
        scratch_shapes=[pltpu.VMEM((5, ROWS, D), BF), pltpu.SemaphoreType.DMA((5,))],
        compiler_params=pltpu.CompilerParams(vmem_limit_bytes=32 << 20),
        cost_estimate=cost(4.2),
    )(core, middle, scale, gain, cotangent, mine, other, *parts)


def feed_kernel(held, order_ref, *refs):
    h_refs, c_ref, weights = refs[:4], refs[4], refs[5:7]
    up_w, packed, down_w, h_all, c_all, total_ref, rows_ref, sems, row_sems, in_sems = refs[-10:]
    outs = refs[7 + held : -10]
    act_refs, grad_refs, out_ref, part_refs = outs[:2], outs[2:4], outs[4], outs[5:]
    first = 4 if held else 0
    copies = []
    for side in range(2):
        for n, (rows, target) in enumerate(
            ((slice(0, SHARD), up_w), (slice(SHARD, SHARD + 96), packed))
        ):
            copy = pltpu.make_async_copy(
                weights[side].at[:, rows], target.at[side], sems.at[side, n]
            )
            copy.start()
            copies.append(copy)
    tokens = fetch(
        [(h_refs[i].at[:ROWS], rows_of(h_all, i)) for i in range(4)]
        + [(c_ref.at[order_ref[first + i]], rows_of(c_all, i)) for i in range(4)],
        in_sems,
    )
    for copy in tokens:
        copy.wait()
    for side in range(2):
        grad_ref = grad_refs[side]
        copies[2 * side].wait()
        up_now = up_w[side].reshape(D, 2 * COLS)
        gate_up = jnp.dot(h_all[...], up_now, preferred_element_type=F32)
        copies[2 * side + 1].wait()
        for g in range(8):
            for (r, c), (rows, cols) in piece_parts():
                down_w[PIECE * g + rows.start : PIECE * g + rows.stop, cols] = packed[side, g, r, c]
        grad_act = contract_cols(c_all[...], down_w[...])
        gate, up = gate_up[:, :COLS], gate_up[:, COLS:]
        sig = jax.nn.sigmoid(gate)
        silu = gate * sig
        act_refs[side][...] = (silu * up).astype(BF)
        rows = jnp.dot(act_refs[side][...], down_w[...], preferred_element_type=F32)
        grad_ref[:, :COLS] = (grad_act * up * sig * (1.0 + gate * (1.0 - sig))).astype(BF)
        grad_ref[:, COLS:] = (grad_act * silu).astype(BF)
        if side == 0:
            total_ref[...] = rows
            part = contract_cols(grad_ref[...], up_now)
        else:
            rows_ref[...] = (total_ref[...] + rows).astype(BF)
            copies = []
            for i in range(4):
                copy = pltpu.make_async_copy(
                    rows_ref.at[ROWS * i : ROWS * (i + 1)],
                    out_ref.at[order_ref[first + i]],
                    row_sems.at[i],
                )
                copy.start()
                copies.append(copy)
            part = part + contract_cols(grad_ref[...], up_now)
            for i in range(4):
                part_refs[i][...] = part[ROWS * i : ROWS * (i + 1)].astype(BF)
            for copy in copies:
                copy.wait()


def feed(order, h_blocks, cot_all, mine, other, held):
    tokens = 4 * ROWS
    at = 1 if held else 0
    widths = (COLS, COLS, 2 * COLS, 2 * COLS)
    outs = pl.pallas_call(
        functools.partial(feed_kernel, len(held)),
        grid=(1,),
        in_specs=scalars(1) + anywhere(7 + len(held)),
        out_specs=[pl.BlockSpec((tokens, w), lambda i: (at, 0)) for w in widths]
        + anywhere(1)
        + whole(4),
        out_shape=[jax.ShapeDtypeStruct((2 * tokens, w), BF) for w in widths]
        + [jax.ShapeDtypeStruct((8, ROWS, D), BF)]
        + [jax.ShapeDtypeStruct((ROWS, D), BF)] * 4,
        scratch_shapes=[
            pltpu.VMEM((2, 8, SHARD, 2 * COLS), BF),
            pltpu.VMEM((2, 8, 96, 2 * COLS), BF),
            pltpu.VMEM((COLS, D), BF),
            pltpu.VMEM((tokens, D), BF),
            pltpu.VMEM((tokens, D), BF),
            pltpu.VMEM((tokens, D), F32),
            pltpu.VMEM((tokens, D), BF),
            pltpu.SemaphoreType.DMA((2, 2)),
            pltpu.SemaphoreType.DMA((4,)),
            pltpu.SemaphoreType.DMA((8,)),
        ],
        input_output_aliases={8 + k: k for k in range(len(held))},
        compiler_params=pltpu.CompilerParams(vmem_limit_bytes=56 << 20),
        cost_estimate=cost(21),
    )(order, *h_blocks, cot_all, mine, other, *held)
    return tuple(outs[:5]), outs[5:]


def assemble_kernel(dq_ref, dkv_ref, branch_ref, cos_ref, sin_ref, both_ref, out_ref):
    dkv = dkv_ref[0].astype(F32)
    for k in range(1, 8):
        dkv = dkv + dkv_ref[k].astype(F32)
    for h in range(2):
        u = dkv[:, HEAD * h : HEAD * (h + 1)]
        u = u * cos_ref[...] - pltpu.roll(u, HEAD // 2, 1) * sin_ref[...]
        u = u.astype(BF)
        both_ref[6, :, HEAD * h : HEAD * (h + 1)] = u
        out_ref[:, WIDTH_Q + HEAD * h : WIDTH_Q + HEAD * (h + 1)] = u
    u = dkv[:, 256:].astype(BF)
    both_ref[7, :, :256] = u
    out_ref[:, WIDTH_Q + 256 :] = u
    for q in range(6):
        u = dq_ref[:, 256 * q : 256 * (q + 1)]
        both_ref[q, :, :256] = u
        out_ref[:, 256 * q : 256 * (q + 1)] = u
        both_ref[q, :, 256:] = branch_ref[:, 256 * q : 256 * (q + 1)]
    for q in range(6, 8):
        both_ref[q, :, 256:] = jnp.zeros((ROWS, 256), BF)


def assemble(dq, dkv, branch, cosine, signed):
    return pl.pallas_call(
        assemble_kernel,
        in_specs=whole(5),
        out_specs=whole(2),
        out_shape=[
            jax.ShapeDtypeStruct((8, ROWS, 512), BF),
            jax.ShapeDtypeStruct((ROWS, QKV), BF),
        ],
        compiler_params=pltpu.CompilerParams(vmem_limit_bytes=16 << 20),
        cost_estimate=cost(1.2),
    )(dq, dkv, branch, cosine, signed)


def on_device(hidden_in, norm_attn, w_qkv, b_qkv, w_out, norm_mlp, w_gate_up, w_down, cotangent):
    core = lax.axis_index("c")
    plane = lax.axis_index(PLANE)
    replica = lax.axis_index(REPLICA)
    group = lax.axis_index(GROUP)
    yl, zz = lax.axis_index("yl"), lax.axis_index("z")
    yh, xx = lax.axis_index("yh"), lax.axis_index("x")
    first_row = group * ROWS
    works = replica < ROLES
    role = jnp.minimum(replica, ROLES - 1)

    x_blocks = send_out(hidden_in[0], PLANE, True)
    pad = jnp.zeros((64,), BF)
    small = jnp.concatenate([b_qkv, norm_attn, pad, norm_mlp, pad]).reshape(3, 256)
    columns = lax.dynamic_slice(w_qkv, (0, plane * 256), (SHARD, 256))
    columns = jnp.concatenate([columns, small, jnp.zeros((13, 256), BF)], axis=0)
    columns = gather_direct(after(columns, *x_blocks[1:5]), GROUP)
    columns = after(columns, *x_blocks[5:])
    qkv_role = columns[:, :SHARD].reshape(D, 256)
    bias_full = columns[:, SHARD : SHARD + 1].astype(F32)
    gain_one = columns[:, SHARD + 1, :SHARD].reshape(1, D).astype(F32)
    gain_two = columns[:, SHARD + 2, :SHARD].reshape(1, D).astype(F32)

    out_half = lax.dynamic_slice(w_out, (0, core * 768), (SHARD, 768))
    out_mine = lax.all_gather(out_half, GROUP, axis=0, tiled=True)
    piece = lax.dynamic_slice(w_down, (role * PIECE, 0), (PIECE, D))
    piece = lax.ppermute(piece, EVERY, down_pairs())
    (packed,) = call(
        pack_kernel,
        1,
        [((SHARD + 96, 2 * COLS), BF)],
        scalars(1) + whole(3),
        works.astype(jnp.int32).reshape(1),
        lax.dynamic_slice(w_gate_up, (0, role * COLS), (SHARD, COLS)),
        lax.dynamic_slice(w_gate_up, (0, FF + role * COLS), (SHARD, COLS)),
        piece,
    )
    feed_mine = lax.all_gather(after(packed, x_blocks[1]), GROUP, axis=0)

    cosine, signed = rope_tables(first_row, ROWS, HEAD)
    turns = plane < 7
    order = jnp.stack([place(yl, zz, o, -1) for o in ALL_OFFSETS]).astype(jnp.int32)
    normed_one_all, heads = project(
        order,
        gain_one,
        qkv_role,
        pick(bias_full, plane),
        jnp.where(turns, cosine, 1.0),
        jnp.where(turns, signed, 0.0),
        x_blocks,
    )

    grad_out = cotangent[0]
    cot_blocks = send_out(after(grad_out, *x_blocks), PLANE, True)
    heads = after(heads, *cot_blocks[1:5])
    heads = lax.all_to_all(heads, PLANE, 0, 0, tiled=True)
    out_other = swap(after(out_mine, heads))
    kv_own = jnp.concatenate([heads[6], heads[7]], axis=1)
    kv_all = gather_direct(kv_own, GROUP)
    kv_all = after(kv_all, *cot_blocks)
    cot_all = arrange(order, cot_blocks)
    me = group.astype(jnp.int32).reshape(1)
    attended, logs = attend(me, heads, kv_all)
    which = core.astype(jnp.int32).reshape(1)
    middle, scale_two, normed_two = middle_of(
        which, attended, hidden_in[0], gain_two, out_mine, out_other
    )

    h_blocks = send_out(normed_two, PLANE)
    feed_other = swap(after(feed_mine, *h_blocks[1:5]))
    qkv_half = lax.dynamic_slice(w_qkv, (0, core * 1024), (SHARD, 1024))
    qkv_mine = lax.all_gather(after(qkv_half, normed_two), GROUP, axis=0, tiled=True)
    held, back_blocks = (), {}
    for part in (slice(0, 4), slice(4, 8)):
        held, parts = feed(order, h_blocks[part], cot_all, feed_mine, feed_other, held)
        for o, block in zip(ALL_OFFSETS[part], parts):
            back_blocks[back(o)] = block
    second_parts, _, round_sums = send_parts(back_blocks, PLANE)

    held_h = after(tuple(h_blocks), parts, qkv_mine)
    given = weight_grads(order, held_h, cot_all, held[3], held[1])
    group_order = jnp.stack([place(yh, xx, o) for o in ALL_OFFSETS]).astype(jnp.int32)
    merged = merged_grads(
        order, group_order, held_h, cot_all, held[2], held[0], swap(given)
    )
    second_parts = after(second_parts, merged)
    grad_middle, grad_branch, grad_attended, gain_two_grad = turning(
        which, middle, scale_two, gain_two, grad_out, out_mine, out_other, second_parts
    )
    grad_q, grad_kv = attend_back(me, heads, kv_all, grad_attended, logs, cosine, signed)
    mlp_parts, mlp_first, _ = send_parts(
        dict(zip(ALL_OFFSETS, merged)), GROUP
    )
    grad_kv = after(grad_kv, *mlp_first)
    grad_kv = lax.all_to_all(grad_kv, GROUP, 0, 0, tiled=True)

    out_rows = after(held[4], *second_parts).reshape(8 * ROWS, D)
    out_rows = lax.psum_scatter(out_rows, PLANE, scatter_dimension=0, tiled=True)
    result = (middle + out_rows.astype(F32)).astype(BF)[None]

    both, grad_projected = assemble(grad_q, grad_kv, grad_branch, cosine, signed)
    qkv_other = swap(after(qkv_mine, both))
    assembled = both
    both = lax.all_to_all(both, PLANE, 0, 0, tiled=True)

    grad_in, gain_one_grad = finish(
        which, grad_projected, qkv_mine, qkv_other, hidden_in[0], gain_one, grad_middle
    )
    keep, give, bias_grad = attention_grads(which, order, normed_one_all, after(both, gain_one_grad, *mlp_parts), h_blocks)
    gains = jnp.stack([gain_one_grad[0], gain_two_grad[0]]).astype(BF).reshape(2, 8, SHARD)
    gains = jnp.pad(gains.transpose(1, 0, 2), ((0, 0), (0, 14), (0, 64)))
    (payload,) = call(
        payload_kernel, 1.4,
        [((8, SHARD + 16, 256), BF)],
        whole(4),
        keep,
        swap(give),
        gains,
        bias_grad,
    )
    mlp_grad = total(after(tuple(mlp_parts), out_rows)).astype(BF)
    down_grad = lax.ppermute(mlp_grad[SHARD:], EVERY, [(t, s) for s, t in down_pairs()])
    mlp_grad = jnp.concatenate([mlp_grad[:SHARD], down_grad], axis=0)
    payload = lax.all_to_all(payload, GROUP, 0, 0, tiled=True)
    grad_blocks = send_out(mlp_grad, PLANE, hold=(payload,))
    other_blocks = [swap(b) for b in grad_blocks[:5]]
    feed_grads = write_grads(which, order, grad_blocks, other_blocks, 0, 5, ())
    other_blocks += [swap(b) for b in after(tuple(grad_blocks[5:]), *feed_grads)]
    gate_up_grad, down_grad = write_grads(which, order, grad_blocks, other_blocks, 5, 8, feed_grads)


    (payload,) = call(sum_kernel, 1, [((8, SHARD + 16, 256), BF)], whole(1), payload)
    mine = lax.all_to_all(payload, PLANE, 0, 0, tiled=True)
    mine = after(mine, *feed_grads)
    other = swap(mine)
    qkv_grad, out_grad, gains, bias_grad = call(
        last_kernel,
        3,
        [((SHARD, QKV), F32), ((SHARD, D), F32), ((16, 256), F32), ((16, 256), F32)],
        [pl.BlockSpec(memory_space=pltpu.SMEM)] * 2 + whole(2),
        which,
        me,
        mine,
        other,
    )

    return (
        result,
        grad_in[None],
        gains[0, :SHARD],
        qkv_grad,
        bias_grad[2],
        out_grad,
        gains[1, :SHARD],
        gate_up_grad,
        down_grad,
    )


def solution(mesh):
    fine = Mesh(mesh.devices.reshape(2, 4, 2, 4, 2), EVERY)
    tokens = P(REPLICA, GROUP, None)
    matrix = P(GROUP, None)
    vector = P(GROUP)
    return jax.shard_map(
        on_device,
        mesh=fine,
        in_specs=(tokens, vector, matrix, vector, matrix, vector, matrix, matrix, tokens),
        out_specs=(tokens, tokens, vector, matrix, vector, matrix, vector, matrix, matrix),
        check_vma=False,
    )
```

```python
import functools

import jax
import jax.numpy as jnp
from jax import lax
from jax.experimental import pallas as pl
from jax.experimental.pallas import tpu as pltpu
from jax.sharding import Mesh, PartitionSpec as P

D = 1536
HEADS = 12
KV_HEADS = 2
HEAD = 128
FF = 8960
QKV = 2048
ROWS = 128
GROUPS = HEADS // KV_HEADS
WIDTH_Q = HEADS * HEAD
WIDTH_K = KV_HEADS * HEAD
ROLES = 14
COLS = FF // ROLES
SHARD = D // 8
PIECE = COLS // 8
PIECES = FF // 8 // PIECE

NORM_EPSILON = 1e-06
ROPE_BASE = 1000000.0
BF = jnp.bfloat16


def cost(micros):
    return pl.CostEstimate(flops=int(micros * SCALE), bytes_accessed=1000, transcendentals=0)


SCALE = 0.58e9
F32 = jnp.float32

GROUP = ("yh", "x")
PLANE = ("yl", "z")
REPLICA = ("yl", "z", "c")
GROUP_CORE = ("yh", "x", "c")
EVERY = ("yh", "x", "yl", "z", "c")

ALL_OFFSETS = ((0, 0), (0, 1), (0, 3), (1, 0), (0, 2), (1, 1), (1, 3), (1, 2))


def shift_pairs(offset):
    dy, dx = offset
    return [
        (y * 4 + x, ((y + dy) % 2) * 4 + (x + dx) % 4) for y in range(2) for x in range(4)
    ]


def back(offset):
    return (offset[0], (4 - offset[1]) % 4)


def send(block, axes, offset):
    return lax.ppermute(block, axes, shift_pairs(offset))


def send_out(block, axes, row=False, hold=()):
    one, three = send(block, axes, (0, 1)), send(block, axes, (0, 3))
    across, two = send(block, axes, (1, 0)), send(block, axes, (0, 2))
    across, two = after((across, two), *hold)
    return [
        block,
        one,
        three,
        across,
        two,
        send(across, axes, (0, 1)),
        send(across, axes, (0, 3)),
        send(across, axes, (0, 2)) if row else send(two, axes, (1, 0)),
    ]


def send_parts(blocks, axes, hold=()):
    first = (
        send(blocks[1, 1], axes, (0, 1)),
        send(blocks[1, 3], axes, (0, 3)),
        send(blocks[1, 2], axes, (1, 0)),
    )
    from_one, from_three, from_across = after(first, *hold)
    two = (blocks[0, 2].astype(F32) + from_across.astype(F32)).astype(BF)
    across = total([blocks[1, 0], from_one, from_three]).astype(BF)
    parts = [
        blocks[0, 0],
        send(blocks[0, 1], axes, (0, 1)),
        send(blocks[0, 3], axes, (0, 3)),
        send(two, axes, (0, 2)),
        send(across, axes, (1, 0)),
    ]
    return parts, first, (two, across)


def after(value, *done):
    return lax.optimization_barrier((value,) + done)[0] if done else value


def total(blocks):
    out = blocks[0].astype(F32)
    for b in blocks[1:]:
        out = out + b.astype(F32)
    return out


def down_pairs():
    pairs = []
    for r in range(ROLES):
        for g in range(8):
            piece = 8 * r + g
            pairs.append(((piece // PIECES) * 16 + piece % PIECES, g * 16 + r))
    return pairs


def rope_tables(first_row, row_count, head_size):
    half_width = head_size // 2
    position = (first_row + jnp.arange(row_count, dtype=jnp.int32)).astype(F32)
    frequency = jnp.power(
        ROPE_BASE, -(jnp.arange(half_width, dtype=jnp.int32).astype(F32) * 2.0) / head_size
    )
    angles = position[:, None] * frequency[None, :]
    cosine = jnp.concatenate([jnp.cos(angles), jnp.cos(angles)], axis=-1)
    signed = jnp.concatenate([-jnp.sin(angles), jnp.sin(angles)], axis=-1)
    return (cosine, signed)


def contract_rows(left_side, right_side):
    return lax.dot_general(
        left_side, right_side, (((0,), (0,)), ((), ())), preferred_element_type=F32
    )


def contract_cols(left_side, right_side):
    return lax.dot_general(
        left_side, right_side, (((1,), (1,)), ((), ())), preferred_element_type=F32
    )


def swap(block):
    return lax.ppermute(block, "c", [(0, 1), (1, 0)])


def gather_direct(block, axes):
    return lax.all_to_all(jnp.broadcast_to(block[None], (8,) + block.shape), axes, 0, 0, tiled=True)


def place(y, x, offset, sign=1):
    return ((y + sign * offset[0]) % 2) * 4 + (x + sign * offset[1]) % 4


def pick(blocks, index):
    return lax.dynamic_index_in_dim(blocks, index, 0, keepdims=False)


def piece_parts():
    for i in range(5):
        for j in range(6):
            low, high = max(96 * i, 80 * j), min(96 * (i + 1), 80 * (j + 1))
            if low < high:
                yield (
                    (slice(low - 96 * i, high - 96 * i), slice(256 * i, 256 * (i + 1))),
                    (slice(low - 80 * j, high - 80 * j), slice(256 * j, 256 * (j + 1))),
                )


def call(kernel, micros, out_shape, in_specs, *args, vmem=48, **more):
    return pl.pallas_call(
        kernel,
        in_specs=in_specs,
        out_specs=[pl.BlockSpec(memory_space=pltpu.VMEM)] * len(out_shape),
        out_shape=[jax.ShapeDtypeStruct(shape, kind) for shape, kind in out_shape],
        compiler_params=pltpu.CompilerParams(vmem_limit_bytes=vmem << 20),
        cost_estimate=cost(micros),
        **more,
    )(*args)


def pack_kernel(works_ref, gate_ref, up_ref, piece_ref, out_ref):
    works = works_ref[0] > 0
    gate, up = gate_ref[...], up_ref[...]
    out_ref[:SHARD, :COLS] = jnp.where(works, gate, jnp.zeros_like(gate))
    out_ref[:SHARD, COLS:] = jnp.where(works, up, jnp.zeros_like(up))
    for (r, c), (rows, cols) in piece_parts():
        out_ref[SHARD + r.start : SHARD + r.stop, c] = piece_ref[rows, cols]


def arrange_kernel(order_ref, *refs):
    for k in range(8):
        refs[8][order_ref[k]] = refs[k][...]


def arrange(order, blocks):
    return call(
        arrange_kernel,
        2,
        [((8,) + blocks[0].shape, BF)],
        [pl.BlockSpec(memory_space=pltpu.SMEM)] + whole(8),
        order,
        *blocks,
    )[0]


def packed_grads(order_ref, refs, up_sum, down_sum, scratch):
    h_all, c_all, grad, act, sems = scratch
    c_ref, grad_ref, act_ref = refs[8:11]
    copies = fetch(
        [(grad_ref, grad)]
        + [(refs[k].at[:ROWS], rows_of(h_all, k)) for k in range(8)]
        + [(act_ref, act)]
        + [(c_ref.at[order_ref[k]], rows_of(c_all, k)) for k in range(8)],
        sems,
    )
    for copy in copies[:9]:
        copy.wait()
    up_sum[...] = contract_rows(h_all[...], grad[...]).reshape(8, SHARD, 2 * COLS).astype(BF)
    for copy in copies[9:]:
        copy.wait()
    down_sum[...] = contract_rows(act[...], c_all[...]).astype(BF)


GRAD_SCRATCH = [
    pltpu.VMEM((8 * ROWS, D), BF),
    pltpu.VMEM((8 * ROWS, D), BF),
    pltpu.VMEM((8 * ROWS, 2 * COLS), BF),
    pltpu.VMEM((8 * ROWS, COLS), BF),
    pltpu.SemaphoreType.DMA((18,)),
]


def weight_kernel(order_ref, *refs):
    out_ref, down_sum = refs[11:13]
    packed_grads(order_ref, refs, out_ref.at[:, :SHARD], down_sum, refs[13:])
    for g in range(8):
        for (r, c), (rows, cols) in piece_parts():
            out_ref[g, SHARD + r.start : SHARD + r.stop, c] = down_sum[
                PIECE * g + rows.start : PIECE * g + rows.stop, cols
            ]


def weight_grads(order, h_blocks, cot_all, grads, acts):
    return call(
        weight_kernel,
        10.7,
        [((8, SHARD + 96, 2 * COLS), BF)],
        scalars(1) + anywhere(11),
        order,
        *h_blocks,
        cot_all,
        grads,
        acts,
        scratch_shapes=[pltpu.VMEM((COLS, D), BF)] + GRAD_SCRATCH,
    )[0]


def merge_kernel(token_order_ref, order_ref, *refs):
    given_ref, outs, (up_sum, down_sum, given, sem) = refs[11], refs[12:20], refs[20:24]
    copy = fetch([(given_ref, given)], sem)[0]
    packed_grads(token_order_ref, refs, up_sum, down_sum, refs[24:])
    copy.wait()
    for k in range(8):
        g = order_ref[k]
        outs[k][:SHARD] = (up_sum[g].astype(F32) + given[g, :SHARD].astype(F32)).astype(BF)
        first = pl.multiple_of(g * PIECE, PIECE)
        for (r, c), (rows, cols) in piece_parts():
            to = slice(SHARD + r.start, SHARD + r.stop)
            own = down_sum[pl.ds(first + rows.start, rows.stop - rows.start), cols]
            outs[k][to, c] = (own.astype(F32) + given[g, to, c].astype(F32)).astype(BF)


def merged_grads(token_order, order, h_blocks, cot_all, grads, acts, given):
    return call(
        merge_kernel,
        15,
        [((SHARD + 96, 2 * COLS), BF)] * 8,
        scalars(2) + anywhere(12),
        token_order,
        order,
        *h_blocks,
        cot_all,
        grads,
        acts,
        given,
        vmem=56,
        scratch_shapes=[
            pltpu.VMEM((8, SHARD, 2 * COLS), BF),
            pltpu.VMEM((COLS, D), BF),
            pltpu.VMEM((8, SHARD + 96, 2 * COLS), BF),
            pltpu.SemaphoreType.DMA((1,)),
        ]
        + GRAD_SCRATCH,
    )


def finish_kernel(
    core_ref, grad_ref, mine_ref, other_ref, x_ref, gain_ref, mid_ref, out_ref, gain_grad_ref
):
    half = QKV // 2
    grad = grad_ref[...]
    mine, other = halves(core_ref, grad[:, :half], grad[:, half:])
    normed = contract_cols(mine, mine_ref[...]) + contract_cols(other, other_ref[...])
    x = x_ref[...].astype(F32)
    scale = lax.rsqrt(jnp.mean(x * x, axis=-1, keepdims=True) + NORM_EPSILON)
    gain_grad_ref[...] = jnp.sum(normed * x * scale, axis=0, keepdims=True)
    weighted = normed * gain_ref[...]
    mean = jnp.mean(weighted * x, axis=-1, keepdims=True)
    out_ref[...] = mid_ref[...] + scale * (weighted - x * (scale * scale * mean))


def finish(core, grad_projected, mine, other, rows, gain, grad_middle):
    return call(
        finish_kernel, 5,
        [((ROWS, D), F32), ((1, D), F32)],
        [pl.BlockSpec(memory_space=pltpu.SMEM)] + whole(6),
        core,
        grad_projected,
        mine,
        other,
        rows,
        gain,
        grad_middle,
    )


def attention_grads_kernel(core_ref, order_ref, normed_ref, both_ref, *refs):
    keep_ref, give_ref, bias_ref, att_all, sems = refs[8:]
    copies = fetch(
        [(refs[k].at[ROWS:], att_all.at[order_ref[k]]) for k in range(8)], sems
    )
    both = both_ref[...].reshape(8 * ROWS, 512)
    role = both[:, :256]
    bias_ref[...] = jnp.sum(role.astype(F32), axis=0, keepdims=True)
    qkv = contract_rows(normed_ref[...].reshape(8 * ROWS, D), role)
    for copy in copies:
        copy.wait()
    out = contract_rows(att_all[...].reshape(8 * ROWS, D), both[:, 256:])
    keep, give = halves(core_ref, qkv, out)
    keep_ref[...] = keep
    give_ref[...] = give.astype(BF)


def attention_grads(core, order, normed, both, bundles):
    return call(
        attention_grads_kernel,
        5,
        [((D, 256), F32), ((D, 256), BF), ((1, 256), F32)],
        scalars(2) + whole(2) + anywhere(8),
        core,
        order,
        normed,
        both,
        *bundles,
        scratch_shapes=[pltpu.VMEM((8, ROWS, D), BF), pltpu.SemaphoreType.DMA((8,))],
    )


def last_kernel(core_ref, group_ref, mine_ref, other_ref, qkv_ref, out_ref, gain_ref, bias_ref):
    gains = jnp.zeros((16, 256), F32)
    for q in range(8):
        mine, other = mine_ref[q].astype(F32), other_ref[q].astype(F32)
        qkv, out = halves(core_ref, mine[:SHARD], other[:SHARD])
        qkv_ref[:, 256 * q : 256 * (q + 1)] = qkv
        if q < 6:
            out_ref[:, 256 * q : 256 * (q + 1)] = out
        gains = gains + mine[SHARD:] + other[SHARD:]
    gain_ref[...] = gains
    g = group_ref[0]
    bias_ref[...] = mine_ref[g, SHARD:].astype(F32) + other_ref[g, SHARD:].astype(F32)


def payload_kernel(keep_ref, other_ref, extra_ref, bias_ref, out_ref):
    row = lax.broadcasted_iota(jnp.int32, (16, 256), 0)
    bias = bias_ref[...].astype(BF).astype(F32)
    for g in range(8):
        rows = slice(SHARD * g, SHARD * (g + 1))
        out_ref[g, :SHARD] = (keep_ref[rows] + other_ref[rows].astype(F32)).astype(BF)
        extra = extra_ref[g].astype(F32)
        out_ref[g, SHARD:] = jnp.where(row == 2, bias, extra).astype(BF)


def sum_kernel(in_ref, out_ref):
    rows = in_ref[0].astype(F32)
    for g in range(1, 8):
        rows = rows + in_ref[g].astype(F32)
    rows = rows.astype(BF)
    for g in range(8):
        out_ref[g] = rows


def write_kernel(low, count, held, core_ref, order_ref, *refs):
    blocks = refs[: 2 * count]
    wide_out, down_out, narrow, wide, down, in_sems, sems = refs[2 * count + held :]
    arrivals = fetch([(blocks[n], narrow.at[n]) for n in range(2 * count)], in_sems)
    for start in (True, False):
        for n in range(2 * count):
            chip = order_ref[low + n % count]
            role = 2 * chip + (core_ref[0] if n < count else 1 - core_ref[0])
            if start:
                arrivals[n].wait()

            @pl.when(chip < ROLES // 2)
            def _(n=n, role=role):
                copies = [
                    pltpu.make_async_copy(
                        wide.at[n, :, :COLS],
                        wide_out.at[:, pl.ds(pl.multiple_of(role * COLS, 128), COLS)],
                        sems.at[n, 0],
                    ),
                    pltpu.make_async_copy(
                        wide.at[n, :, COLS:],
                        wide_out.at[:, pl.ds(pl.multiple_of(FF + role * COLS, 128), COLS)],
                        sems.at[n, 1],
                    ),
                    pltpu.make_async_copy(
                        down.at[n],
                        down_out.at[pl.ds(pl.multiple_of(role * PIECE, PIECE), PIECE)],
                        sems.at[n, 2],
                    ),
                ]
                if start:
                    wide[n] = narrow[n, :SHARD].astype(F32)
                    copies[0].start()
                    copies[1].start()
                    for (r, c), (rows, cols) in piece_parts():
                        down[n, rows, cols] = narrow[
                            n, SHARD + r.start : SHARD + r.stop, c
                        ].astype(F32)
                    copies[2].start()
                else:
                    for copy in copies:
                        copy.wait()


def write_grads(core, order, mine, other, low, high, held):
    count = high - low
    return pl.pallas_call(
        functools.partial(write_kernel, low, count, len(held)),
        in_specs=scalars(2) + anywhere(2 * count + len(held)),
        out_specs=anywhere(2),
        out_shape=[
            jax.ShapeDtypeStruct((SHARD, 2 * FF), F32),
            jax.ShapeDtypeStruct((FF // 8, D), F32),
        ],
        scratch_shapes=[
            pltpu.VMEM((2 * count, SHARD + 96, 2 * COLS), BF),
            pltpu.VMEM((2 * count, SHARD, 2 * COLS), F32),
            pltpu.VMEM((2 * count, PIECE, D), F32),
            pltpu.SemaphoreType.DMA((2 * count,)),
            pltpu.SemaphoreType.DMA((2 * count, 3)),
        ],
        input_output_aliases={2 + 2 * count + k: k for k in range(len(held))},
        compiler_params=pltpu.CompilerParams(vmem_limit_bytes=48 << 20),
        cost_estimate=cost(2 * count),
    )(core, order, *mine[low:high], *other[low:high], *held)


def project_kernel(order_ref, gain_ref, w_ref, bias_ref, cos_ref, sin_ref, *refs):
    normed_ref, heads_ref, x_all, sems = refs[8:]
    copies = fetch([(refs[k], x_all.at[k]) for k in range(8)], sems)
    for k in range(8):
        copies[k].wait()
        rows = x_all[k].astype(F32)
        scale = lax.rsqrt(jnp.mean(rows * rows, axis=-1, keepdims=True) + NORM_EPSILON)
        normed = (rows * scale * gain_ref[...]).astype(BF)
        at = order_ref[k]
        normed_ref[at] = normed
        out = jnp.dot(normed, w_ref[...], preferred_element_type=F32) + bias_ref[...]
        for h in range(2):
            u = out[:, HEAD * h : HEAD * (h + 1)]
            u = u * cos_ref[...] + pltpu.roll(u, HEAD // 2, 1) * sin_ref[...]
            heads_ref[at, :, HEAD * h : HEAD * (h + 1)] = u.astype(BF)


def whole(count):
    return [pl.BlockSpec(memory_space=pltpu.VMEM)] * count


def scalars(count):
    return [pl.BlockSpec(memory_space=pltpu.SMEM)] * count


def anywhere(count):
    return [pl.BlockSpec(memory_space=pl.ANY)] * count


def fetch(pairs, sems):
    copies = [
        pltpu.make_async_copy(source, target, sems.at[k]) for k, (source, target) in enumerate(pairs)
    ]
    for copy in copies:
        copy.start()
    return copies


def rows_of(ref, k):
    return ref.at[ROWS * k : ROWS * (k + 1)]


def project(order, gain, weight, bias, cosine, signed, blocks):
    return pl.pallas_call(
        project_kernel,
        in_specs=scalars(1) + whole(5) + anywhere(8),
        out_specs=whole(2),
        out_shape=[
            jax.ShapeDtypeStruct((8, ROWS, D), BF),
            jax.ShapeDtypeStruct((8, ROWS, 256), BF),
        ],
        scratch_shapes=[pltpu.VMEM((8, ROWS, D), BF), pltpu.SemaphoreType.DMA((8,))],
        compiler_params=pltpu.CompilerParams(vmem_limit_bytes=32 << 20),
        cost_estimate=cost(4),
    )(order, gain, weight, bias, cosine, signed, *blocks)


def head_stack(ref, side):
    return jnp.concatenate(
        [
            ref[h // 2, :, HEAD * (h % 2) : HEAD * (h % 2 + 1)]
            for h in range(GROUPS * side, GROUPS * (side + 1))
        ],
        axis=0,
    )


def scores_of(me_ref, queries, keys):
    raw = lax.dot_general(
        queries, keys, (((1,), (1,)), ((), ())), preferred_element_type=F32
    )
    raw = raw.reshape(GROUPS, ROWS, 8 * ROWS) * HEAD ** (-0.5)
    row = me_ref[0] * ROWS + lax.broadcasted_iota(jnp.int32, (ROWS, 8 * ROWS), 0)
    col = lax.broadcasted_iota(jnp.int32, (ROWS, 8 * ROWS), 1)
    return jnp.where((col <= row)[None], raw, -1e30)


def attend_kernel(me_ref, heads_ref, kv_ref, out_ref, log_ref):
    kv = kv_ref[...].reshape(8 * ROWS, 512)
    for side in range(2):
        keys = kv[:, HEAD * side : HEAD * (side + 1)]
        values = kv[:, 256 + HEAD * side : 256 + HEAD * (side + 1)]
        scores = scores_of(me_ref, head_stack(heads_ref, side), keys)
        top = jnp.max(scores, axis=-1, keepdims=True)
        exponent = jnp.exp(scores - top)
        row_total = jnp.sum(exponent, axis=-1, keepdims=True)
        mixed = jnp.dot(
            exponent.astype(BF).reshape(GROUPS * ROWS, 8 * ROWS),
            values,
            preferred_element_type=F32,
        ).reshape(GROUPS, ROWS, HEAD)
        mixed = mixed / row_total
        logs = top + jnp.log(row_total)
        for i in range(GROUPS):
            h = GROUPS * side + i
            out_ref[:, HEAD * h : HEAD * (h + 1)] = mixed[i].astype(BF)
            log_ref[h] = logs[i]


def attend(me, heads, kv):
    return pl.pallas_call(
        attend_kernel,
        in_specs=[pl.BlockSpec(memory_space=pltpu.SMEM)] + whole(2),
        out_specs=whole(2),
        out_shape=[
            jax.ShapeDtypeStruct((ROWS, WIDTH_Q), BF),
            jax.ShapeDtypeStruct((HEADS, ROWS, 1), F32),
        ],
        compiler_params=pltpu.CompilerParams(vmem_limit_bytes=48 << 20),
        cost_estimate=cost(5),
    )(me, heads, kv)


def attend_back_kernel(
    me_ref, heads_ref, kv_ref, grad_ref, log_ref, cos_ref, sin_ref, dq_ref, dkv_ref
):
    kv = kv_ref[...].reshape(8 * ROWS, 512)
    for side in range(2):
        keys = kv[:, HEAD * side : HEAD * (side + 1)]
        values = kv[:, 256 + HEAD * side : 256 + HEAD * (side + 1)]
        queries = head_stack(heads_ref, side)
        grads = jnp.concatenate(
            [
                grad_ref[:, HEAD * h : HEAD * (h + 1)]
                for h in range(GROUPS * side, GROUPS * (side + 1))
            ],
            axis=0,
        )
        scores = scores_of(me_ref, queries, keys)
        probs = jnp.exp(scores - log_ref[GROUPS * side : GROUPS * (side + 1)])
        grad_probs = contract_cols(grads, values).reshape(GROUPS, ROWS, 8 * ROWS)
        inner = jnp.sum(probs * grad_probs, axis=-1, keepdims=True)
        grad_scores = (probs * (grad_probs - inner)).astype(BF)
        grad_scores = grad_scores.reshape(GROUPS * ROWS, 8 * ROWS)
        probs_low = probs.astype(BF).reshape(GROUPS * ROWS, 8 * ROWS)
        dq = jnp.dot(grad_scores, keys, preferred_element_type=F32) * HEAD ** (-0.5)
        dk = contract_rows(grad_scores, queries) * HEAD ** (-0.5)
        dv = contract_rows(probs_low, grads)
        for i in range(GROUPS):
            h = GROUPS * side + i
            u = dq[ROWS * i : ROWS * (i + 1)]
            u = u * cos_ref[...] - pltpu.roll(u, HEAD // 2, 1) * sin_ref[...]
            dq_ref[:, HEAD * h : HEAD * (h + 1)] = u.astype(BF)
        low, high = HEAD * side, HEAD * (side + 1)
        dkv_ref[:, :, low:high] = dk.astype(BF).reshape(8, ROWS, HEAD)
        dkv_ref[:, :, 256 + low : 256 + high] = dv.astype(BF).reshape(8, ROWS, HEAD)


def attend_back(me, heads, kv, grads, logs, cosine, signed):
    return pl.pallas_call(
        attend_back_kernel,
        in_specs=[pl.BlockSpec(memory_space=pltpu.SMEM)] + whole(6),
        out_specs=whole(2),
        out_shape=[
            jax.ShapeDtypeStruct((ROWS, WIDTH_Q), BF),
            jax.ShapeDtypeStruct((8, ROWS, 512), BF),
        ],
        compiler_params=pltpu.CompilerParams(vmem_limit_bytes=56 << 20),
        cost_estimate=cost(9),
    )(me, heads, kv, grads, logs, cosine, signed)


def halves(core_ref, mine, other):
    first = core_ref[0] == 0
    return jnp.where(first, mine, other), jnp.where(first, other, mine)


def middle_kernel(
    core_ref, att_ref, x_ref, gain_ref, mine_ref, other_ref, mid_ref, scale_ref, h_ref
):
    att = att_ref[...]
    mine = jnp.dot(att, mine_ref[...], preferred_element_type=F32)
    other = jnp.dot(att, other_ref[...], preferred_element_type=F32)
    low, high = halves(core_ref, mine, other)
    low = x_ref[:, : D // 2].astype(F32) + low
    high = x_ref[:, D // 2 :].astype(F32) + high
    square = jnp.sum(low * low, axis=-1, keepdims=True) + jnp.sum(
        high * high, axis=-1, keepdims=True
    )
    scale = lax.rsqrt(square / D + NORM_EPSILON)
    scale_ref[...] = scale
    mid_ref[:, : D // 2] = low
    mid_ref[:, D // 2 :] = high
    h_ref[:ROWS, : D // 2] = (low * scale * gain_ref[:, : D // 2]).astype(BF)
    h_ref[:ROWS, D // 2 :] = (high * scale * gain_ref[:, D // 2 :]).astype(BF)
    h_ref[ROWS:] = att


def middle_of(core, attended, rows, gain, mine, other):
    return pl.pallas_call(
        middle_kernel,
        in_specs=[pl.BlockSpec(memory_space=pltpu.SMEM)]
        + whole(5),
        out_specs=whole(3),
        out_shape=[
            jax.ShapeDtypeStruct((ROWS, D), F32),
            jax.ShapeDtypeStruct((ROWS, 1), F32),
            jax.ShapeDtypeStruct((2 * ROWS, D), BF),
        ],
        compiler_params=pltpu.CompilerParams(vmem_limit_bytes=24 << 20),
        cost_estimate=cost(3),
    )(core, attended, rows, gain, mine, other)


def turning_kernel(core_ref, mid_ref, scale_ref, gain_ref, cot_ref, mine_ref, other_ref, *refs):
    mid_grad_ref, branch_ref, att_ref, gain_grad_ref, arrived, sems = refs[5:]
    copies = fetch([(refs[k], arrived.at[k]) for k in range(5)], sems)
    for copy in copies:
        copy.wait()
    grad = arrived[0].astype(F32)
    for k in range(1, 5):
        grad = grad + arrived[k].astype(F32)
    mid, scale = mid_ref[...], scale_ref[...]
    gain_grad_ref[...] = jnp.sum(grad * mid * scale, axis=0, keepdims=True)
    weighted = grad * gain_ref[...]
    mean = jnp.mean(weighted * mid, axis=-1, keepdims=True)
    grad = cot_ref[...].astype(F32) + scale * (weighted - mid * (scale * scale * mean))
    mid_grad_ref[...] = grad
    branch = grad.astype(BF)
    branch_ref[...] = branch
    mine, other = halves(core_ref, branch[:, : D // 2], branch[:, D // 2 :])
    att = contract_cols(mine, mine_ref[...]) + contract_cols(other, other_ref[...])
    att_ref[...] = att.astype(BF)


def turning(core, middle, scale, gain, cotangent, mine, other, parts):
    return pl.pallas_call(
        turning_kernel,
        in_specs=[pl.BlockSpec(memory_space=pltpu.SMEM)]
        + whole(6)
        + anywhere(5),
        out_specs=whole(4),
        out_shape=[
            jax.ShapeDtypeStruct((ROWS, D), F32),
            jax.ShapeDtypeStruct((ROWS, D), BF),
            jax.ShapeDtypeStruct((ROWS, D), BF),
            jax.ShapeDtypeStruct((1, D), F32),
        ],
        scratch_shapes=[pltpu.VMEM((5, ROWS, D), BF), pltpu.SemaphoreType.DMA((5,))],
        compiler_params=pltpu.CompilerParams(vmem_limit_bytes=32 << 20),
        cost_estimate=cost(4.2),
    )(core, middle, scale, gain, cotangent, mine, other, *parts)


def feed_kernel(held, order_ref, *refs):
    h_refs, c_ref, weights = refs[:4], refs[4], refs[5:7]
    up_w, packed, down_w, h_all, c_all, total_ref, rows_ref, sems, row_sems, in_sems = refs[-10:]
    outs = refs[7 + held : -10]
    act_refs, grad_refs, out_ref, part_refs = outs[:2], outs[2:4], outs[4], outs[5:]
    first = 4 if held else 0
    copies = []
    for side in range(2):
        for n, (rows, target) in enumerate(
            ((slice(0, SHARD), up_w), (slice(SHARD, SHARD + 96), packed))
        ):
            copy = pltpu.make_async_copy(
                weights[side].at[:, rows], target.at[side], sems.at[side, n]
            )
            copy.start()
            copies.append(copy)
    tokens = fetch(
        [(h_refs[i].at[:ROWS], rows_of(h_all, i)) for i in range(4)]
        + [(c_ref.at[order_ref[first + i]], rows_of(c_all, i)) for i in range(4)],
        in_sems,
    )
    for copy in tokens:
        copy.wait()
    for side in range(2):
        grad_ref = grad_refs[side]
        copies[2 * side].wait()
        up_now = up_w[side].reshape(D, 2 * COLS)
        gate_up = jnp.dot(h_all[...], up_now, preferred_element_type=F32)
        copies[2 * side + 1].wait()
        for g in range(8):
            for (r, c), (rows, cols) in piece_parts():
                down_w[PIECE * g + rows.start : PIECE * g + rows.stop, cols] = packed[side, g, r, c]
        grad_act = contract_cols(c_all[...], down_w[...])
        gate, up = gate_up[:, :COLS], gate_up[:, COLS:]
        sig = jax.nn.sigmoid(gate)
        silu = gate * sig
        act_refs[side][...] = (silu * up).astype(BF)
        rows = jnp.dot(act_refs[side][...], down_w[...], preferred_element_type=F32)
        grad_ref[:, :COLS] = (grad_act * up * sig * (1.0 + gate * (1.0 - sig))).astype(BF)
        grad_ref[:, COLS:] = (grad_act * silu).astype(BF)
        if side == 0:
            total_ref[...] = rows
            part = contract_cols(grad_ref[...], up_now)
        else:
            rows_ref[...] = (total_ref[...] + rows).astype(BF)
            copies = []
            for i in range(4):
                copy = pltpu.make_async_copy(
                    rows_ref.at[ROWS * i : ROWS * (i + 1)],
                    out_ref.at[order_ref[first + i]],
                    row_sems.at[i],
                )
                copy.start()
                copies.append(copy)
            part = part + contract_cols(grad_ref[...], up_now)
            for i in range(4):
                part_refs[i][...] = part[ROWS * i : ROWS * (i + 1)].astype(BF)
            for copy in copies:
                copy.wait()


def feed(order, h_blocks, cot_all, mine, other, held):
    tokens = 4 * ROWS
    at = 1 if held else 0
    widths = (COLS, COLS, 2 * COLS, 2 * COLS)
    outs = pl.pallas_call(
        functools.partial(feed_kernel, len(held)),
        grid=(1,),
        in_specs=scalars(1) + anywhere(7 + len(held)),
        out_specs=[pl.BlockSpec((tokens, w), lambda i: (at, 0)) for w in widths]
        + anywhere(1)
        + whole(4),
        out_shape=[jax.ShapeDtypeStruct((2 * tokens, w), BF) for w in widths]
        + [jax.ShapeDtypeStruct((8, ROWS, D), BF)]
        + [jax.ShapeDtypeStruct((ROWS, D), BF)] * 4,
        scratch_shapes=[
            pltpu.VMEM((2, 8, SHARD, 2 * COLS), BF),
            pltpu.VMEM((2, 8, 96, 2 * COLS), BF),
            pltpu.VMEM((COLS, D), BF),
            pltpu.VMEM((tokens, D), BF),
            pltpu.VMEM((tokens, D), BF),
            pltpu.VMEM((tokens, D), F32),
            pltpu.VMEM((tokens, D), BF),
            pltpu.SemaphoreType.DMA((2, 2)),
            pltpu.SemaphoreType.DMA((4,)),
            pltpu.SemaphoreType.DMA((8,)),
        ],
        input_output_aliases={8 + k: k for k in range(len(held))},
        compiler_params=pltpu.CompilerParams(vmem_limit_bytes=56 << 20),
        cost_estimate=cost(21),
    )(order, *h_blocks, cot_all, mine, other, *held)
    return tuple(outs[:5]), outs[5:]


def assemble_kernel(dq_ref, dkv_ref, branch_ref, cos_ref, sin_ref, both_ref, out_ref):
    dkv = dkv_ref[0].astype(F32)
    for k in range(1, 8):
        dkv = dkv + dkv_ref[k].astype(F32)
    for h in range(2):
        u = dkv[:, HEAD * h : HEAD * (h + 1)]
        u = u * cos_ref[...] - pltpu.roll(u, HEAD // 2, 1) * sin_ref[...]
        u = u.astype(BF)
        both_ref[6, :, HEAD * h : HEAD * (h + 1)] = u
        out_ref[:, WIDTH_Q + HEAD * h : WIDTH_Q + HEAD * (h + 1)] = u
    u = dkv[:, 256:].astype(BF)
    both_ref[7, :, :256] = u
    out_ref[:, WIDTH_Q + 256 :] = u
    for q in range(6):
        u = dq_ref[:, 256 * q : 256 * (q + 1)]
        both_ref[q, :, :256] = u
        out_ref[:, 256 * q : 256 * (q + 1)] = u
        both_ref[q, :, 256:] = branch_ref[:, 256 * q : 256 * (q + 1)]
    for q in range(6, 8):
        both_ref[q, :, 256:] = jnp.zeros((ROWS, 256), BF)


def assemble(dq, dkv, branch, cosine, signed):
    return pl.pallas_call(
        assemble_kernel,
        in_specs=whole(5),
        out_specs=whole(2),
        out_shape=[
            jax.ShapeDtypeStruct((8, ROWS, 512), BF),
            jax.ShapeDtypeStruct((ROWS, QKV), BF),
        ],
        compiler_params=pltpu.CompilerParams(vmem_limit_bytes=16 << 20),
        cost_estimate=cost(1.2),
    )(dq, dkv, branch, cosine, signed)


def on_device(hidden_in, norm_attn, w_qkv, b_qkv, w_out, norm_mlp, w_gate_up, w_down, cotangent):
    core = lax.axis_index("c")
    plane = lax.axis_index(PLANE)
    replica = lax.axis_index(REPLICA)
    group = lax.axis_index(GROUP)
    yl, zz = lax.axis_index("yl"), lax.axis_index("z")
    yh, xx = lax.axis_index("yh"), lax.axis_index("x")
    first_row = group * ROWS
    works = replica < ROLES
    role = jnp.minimum(replica, ROLES - 1)

    x_blocks = send_out(hidden_in[0], PLANE, True)
    pad = jnp.zeros((64,), BF)
    small = jnp.concatenate([b_qkv, norm_attn, pad, norm_mlp, pad]).reshape(3, 256)
    columns = lax.dynamic_slice(w_qkv, (0, plane * 256), (SHARD, 256))
    columns = jnp.concatenate([columns, small, jnp.zeros((13, 256), BF)], axis=0)
    columns = gather_direct(after(columns, *x_blocks[1:5]), GROUP)
    columns = after(columns, *x_blocks[5:])
    qkv_role = columns[:, :SHARD].reshape(D, 256)
    bias_full = columns[:, SHARD : SHARD + 1].astype(F32)
    gain_one = columns[:, SHARD + 1, :SHARD].reshape(1, D).astype(F32)
    gain_two = columns[:, SHARD + 2, :SHARD].reshape(1, D).astype(F32)

    out_half = lax.dynamic_slice(w_out, (0, core * 768), (SHARD, 768))
    out_mine = lax.all_gather(out_half, GROUP, axis=0, tiled=True)
    piece = lax.dynamic_slice(w_down, (role * PIECE, 0), (PIECE, D))
    piece = lax.ppermute(piece, EVERY, down_pairs())
    (packed,) = call(
        pack_kernel,
        1,
        [((SHARD + 96, 2 * COLS), BF)],
        scalars(1) + whole(3),
        works.astype(jnp.int32).reshape(1),
        lax.dynamic_slice(w_gate_up, (0, role * COLS), (SHARD, COLS)),
        lax.dynamic_slice(w_gate_up, (0, FF + role * COLS), (SHARD, COLS)),
        piece,
    )
    feed_mine = lax.all_gather(after(packed, x_blocks[1]), GROUP, axis=0)

    cosine, signed = rope_tables(first_row, ROWS, HEAD)
    turns = plane < 7
    order = jnp.stack([place(yl, zz, o, -1) for o in ALL_OFFSETS]).astype(jnp.int32)
    normed_one_all, heads = project(
        order,
        gain_one,
        qkv_role,
        pick(bias_full, plane),
        jnp.where(turns, cosine, 1.0),
        jnp.where(turns, signed, 0.0),
        x_blocks,
    )

    grad_out = cotangent[0]
    cot_blocks = send_out(after(grad_out, *x_blocks), PLANE, True)
    heads = after(heads, *cot_blocks[1:5])
    heads = lax.all_to_all(heads, PLANE, 0, 0, tiled=True)
    out_other = swap(after(out_mine, heads))
    kv_own = jnp.concatenate([heads[6], heads[7]], axis=1)
    kv_all = gather_direct(kv_own, GROUP)
    kv_all = after(kv_all, *cot_blocks)
    cot_all = arrange(order, cot_blocks)
    me = group.astype(jnp.int32).reshape(1)
    attended, logs = attend(me, heads, kv_all)
    which = core.astype(jnp.int32).reshape(1)
    middle, scale_two, normed_two = middle_of(
        which, attended, hidden_in[0], gain_two, out_mine, out_other
    )

    h_blocks = send_out(normed_two, PLANE)
    feed_other = swap(after(feed_mine, *h_blocks[3:5]))
    qkv_half = lax.dynamic_slice(w_qkv, (0, core * 1024), (SHARD, 1024))
    qkv_mine = lax.all_gather(after(qkv_half, normed_two), GROUP, axis=0, tiled=True)
    held, back_blocks = (), {}
    for part in (slice(0, 4), slice(4, 8)):
        held, parts = feed(order, h_blocks[part], cot_all, feed_mine, feed_other, held)
        for o, block in zip(ALL_OFFSETS[part], parts):
            back_blocks[back(o)] = block
    second_parts, _, round_sums = send_parts(back_blocks, PLANE)

    held_h = after(tuple(h_blocks), parts, qkv_mine)
    given = weight_grads(order, held_h, cot_all, held[3], held[1])
    group_order = jnp.stack([place(yh, xx, o) for o in ALL_OFFSETS]).astype(jnp.int32)
    merged = merged_grads(
        order, group_order, held_h, cot_all, held[2], held[0], swap(given)
    )
    second_parts = after(second_parts, merged)
    grad_middle, grad_branch, grad_attended, gain_two_grad = turning(
        which, middle, scale_two, gain_two, grad_out, out_mine, out_other, second_parts
    )
    grad_q, grad_kv = attend_back(me, heads, kv_all, grad_attended, logs, cosine, signed)
    mlp_parts, mlp_first, _ = send_parts(
        dict(zip(ALL_OFFSETS, merged)), GROUP
    )
    grad_kv = after(grad_kv, *mlp_first)
    grad_kv = lax.all_to_all(grad_kv, GROUP, 0, 0, tiled=True)

    out_rows = after(held[4], *second_parts).reshape(8 * ROWS, D)
    out_rows = lax.psum_scatter(out_rows, PLANE, scatter_dimension=0, tiled=True)
    result = (middle + out_rows.astype(F32)).astype(BF)[None]

    both, grad_projected = assemble(grad_q, grad_kv, grad_branch, cosine, signed)
    qkv_other = swap(after(qkv_mine, both))
    assembled = both
    both = lax.all_to_all(both, PLANE, 0, 0, tiled=True)

    grad_in, gain_one_grad = finish(
        which, grad_projected, qkv_mine, qkv_other, hidden_in[0], gain_one, grad_middle
    )
    keep, give, bias_grad = attention_grads(which, order, normed_one_all, after(both, gain_one_grad, *mlp_parts), h_blocks)
    gains = jnp.stack([gain_one_grad[0], gain_two_grad[0]]).astype(BF).reshape(2, 8, SHARD)
    gains = jnp.pad(gains.transpose(1, 0, 2), ((0, 0), (0, 14), (0, 64)))
    (payload,) = call(
        payload_kernel, 1.4,
        [((8, SHARD + 16, 256), BF)],
        whole(4),
        keep,
        swap(give),
        gains,
        bias_grad,
    )
    mlp_grad = total(after(tuple(mlp_parts), out_rows)).astype(BF)
    down_grad = lax.ppermute(mlp_grad[SHARD:], EVERY, [(t, s) for s, t in down_pairs()])
    mlp_grad = jnp.concatenate([mlp_grad[:SHARD], down_grad], axis=0)
    payload = lax.all_to_all(payload, GROUP, 0, 0, tiled=True)
    grad_blocks = send_out(mlp_grad, PLANE, hold=(payload,))
    other_blocks = [swap(b) for b in grad_blocks[:5]]
    feed_grads = write_grads(which, order, grad_blocks, other_blocks, 0, 5, ())
    other_blocks += [swap(b) for b in after(tuple(grad_blocks[5:]), *feed_grads)]
    gate_up_grad, down_grad = write_grads(which, order, grad_blocks, other_blocks, 5, 8, feed_grads)


    (payload,) = call(sum_kernel, 1, [((8, SHARD + 16, 256), BF)], whole(1), payload)
    mine = lax.all_to_all(payload, PLANE, 0, 0, tiled=True)
    mine = after(mine, *feed_grads)
    other = swap(mine)
    qkv_grad, out_grad, gains, bias_grad = call(
        last_kernel,
        3,
        [((SHARD, QKV), F32), ((SHARD, D), F32), ((16, 256), F32), ((16, 256), F32)],
        [pl.BlockSpec(memory_space=pltpu.SMEM)] * 2 + whole(2),
        which,
        me,
        mine,
        other,
    )

    return (
        result,
        grad_in[None],
        gains[0, :SHARD],
        qkv_grad,
        bias_grad[2],
        out_grad,
        gains[1, :SHARD],
        gate_up_grad,
        down_grad,
    )


def solution(mesh):
    fine = Mesh(mesh.devices.reshape(2, 4, 2, 4, 2), EVERY)
    tokens = P(REPLICA, GROUP, None)
    matrix = P(GROUP, None)
    vector = P(GROUP)
    return jax.shard_map(
        on_device,
        mesh=fine,
        in_specs=(tokens, vector, matrix, vector, matrix, vector, matrix, matrix, tokens),
        out_specs=(tokens, tokens, vector, matrix, vector, matrix, vector, matrix, matrix),
        check_vma=False,
    )
```
